32 devices in a mesh: groups: 2 (over x), rows: 8 (over z, y), cols: 2 (over core).
Axes of the slice: x: 2, y: 2, z: 4, core: 2. Of those that a mesh axis runs over, the one named last changes fastest.
Arguments:
- embeddings: bfloat16 [16384, 1024], P(('groups', 'rows', 'cols')), parts along dimension 0
- pair_list: int32 [16, 63, 2], P(('rows', 'cols')), may hold values from 0 to 31, as said below
- pair_count: int32 [16], P(('rows', 'cols')), may hold values from 1 to 63, as said below
Outputs:
- best_match: float32 [16384], P(('groups', 'rows', 'cols')), parts along dimension 0
The draws below stay inside these ranges and needn't reach their ends.
There are 2 independent parts, one for each index of `groups`. The reference program is written for one: setup_inputs(seed, part) draws one part's arguments, and reference() takes and returns one part's arrays. A program takes and returns all parts, laid end to end along the dimension named above; an argument that names none is the same for every part. Nothing has to cross between parts.
Inputs may be any that keep to these rules, and one draw needn't show every extreme that they name: `pair_list`: device d = r * (devices along cols) + c lists pairs (a, b) with a among blocks r * 4 to r * 4 + 3 and b a block held by a device of cols index c, where device e holds blocks e * 2 to e * 2 + 1. Every pair of blocks a <= b appears exactly once over all devices, as (a, b) or (b, a). Entries past a device's count are zero. `pair_count`: some device holds exactly 63 pairs.
All inputs are finite; a program needn't handle non-finite values.
Results may differ from the reference program's by a relative error of at most 0.00051.
Values may be sent and summed in bfloat16 or wider, within the bound.
A program may use at most 128 MiB of HBM per device.

```python
import jax
import jax.numpy as jnp
from jax import lax

D = 1024
BLK = 256
BLK_DEV = 2
NDEV = 16
NBLK = 32
ROWS = 8192
BAND = 4
CAP = 63


def assign_pairs(key):
    key_coin, key_pick = jax.random.split(key)
    col_devs = BAND // BLK_DEV
    first_ids = jnp.broadcast_to(jnp.arange(NBLK, dtype=jnp.int32)[:, None], (NBLK, NBLK))
    second_ids = jnp.transpose(first_ids)

    def tile_of(row_blk, col_blk):
        return row_blk // BAND * col_devs + col_blk // BLK_DEV % col_devs
    forward = tile_of(first_ids, second_ids)
    backward = tile_of(second_ids, first_ids)
    chosen = jax.random.randint(key_pick, (), 0, NDEV, dtype=jnp.int32)
    forward_coin = jax.random.randint(key_coin, (NBLK, NBLK), 0, 4, dtype=jnp.int32) > 0
    take_forward = (forward_coin | (forward == chosen)) & jnp.logical_not((backward == chosen) & (forward != chosen))
    owner_ids = jnp.where(take_forward, forward, backward)
    owner_ids = jnp.where(first_ids <= second_ids, owner_ids, NDEV).reshape(-1).astype(jnp.int32)
    row_pick = jnp.where(take_forward, first_ids, second_ids).reshape(-1)
    col_pick = jnp.where(take_forward, second_ids, first_ids).reshape(-1)
    positions = jnp.arange(NBLK * NBLK, dtype=jnp.int32)
    sorted_at = jnp.argsort(owner_ids * (NBLK * NBLK) + positions, stable=True)
    sorted_owner = owner_ids[sorted_at]
    counts = jnp.sum((owner_ids[None, :] == jnp.arange(NDEV, dtype=jnp.int32)[:, None]).astype(jnp.int32), axis=1)
    offsets = jnp.cumsum(counts) - counts
    offsets_pad = jnp.concatenate([offsets, jnp.zeros((1,), jnp.int32)])
    slot_ids = positions - offsets_pad[sorted_owner]
    pair_ids = jnp.stack([row_pick[sorted_at], col_pick[sorted_at]], axis=1)
    table = jnp.zeros((NDEV, CAP, 2), jnp.int32).at[sorted_owner, slot_ids].set(pair_ids, mode='drop')
    return (table, counts.astype(jnp.int32))


def draw_pair_list(key, part):
    return assign_pairs(key)[0]


def draw_pair_count(key, part):
    return assign_pairs(key)[1]


def draw_embeddings(key, part):
    key = jax.random.fold_in(key, 11)
    key_perm, key_base, key_jit, key_spread, key_scale, key_twin = jax.random.split(key, 6)
    twin_pairs = 3 * ROWS // 20
    base_total = ROWS - twin_pairs
    shuffle = jax.random.permutation(key_perm, ROWS)
    rank_ids = jnp.argsort(shuffle, stable=True).astype(jnp.int32)
    is_twin = rank_ids < 2 * twin_pairs
    base_ids = jnp.where(is_twin, rank_ids // 2, rank_ids - twin_pairs).astype(jnp.int32)
    spread = jnp.exp(jax.random.uniform(key_spread, (base_total, 1), jnp.float32, jnp.log(0.9), jnp.log(1.1)))
    twin_width = jnp.exp(jax.random.uniform(key_twin, (ROWS, 1), jnp.float32, jnp.log(0.1), jnp.log(0.45)))
    twin_width = jnp.where(is_twin[:, None], twin_width, 0.0)
    row_scale = jnp.exp(jax.random.uniform(key_scale, (ROWS, 1), jnp.float32, 0.0, jnp.log(10.0)))
    noise = jax.random.normal(key_base, (base_total, D), jnp.float32)
    jitter = jax.random.normal(key_jit, (ROWS, D), jnp.float32)
    bases = spread * noise
    result = (bases[base_ids] + twin_width * jitter) * row_scale
    return result.astype(jnp.bfloat16)


def setup_inputs(seed: int = 0, part: int = 0) -> dict:
    key_list = jax.random.split(jax.random.key(seed), 4)
    part_keys = jax.random.split(jax.random.fold_in(key_list[3], part), 4)
    return {
        "embeddings": draw_embeddings(jax.random.fold_in(jax.random.fold_in(key_list[3], part), 71), part),
        "pair_list": draw_pair_list(jax.random.fold_in(key_list[3], 71), part),
        "pair_count": draw_pair_count(jax.random.fold_in(key_list[3], 71), part),
    }


lowest = -3.0
epsilon = 1e-06

def reference(embeddings, pair_list, pair_count):
    values = embeddings.astype(jnp.float32)
    unit_rows = (values * lax.rsqrt(lax.optimization_barrier(jnp.mean(values * values, axis=1, keepdims=True)) + epsilon) * D ** (-0.5)).astype(jnp.bfloat16)
    blocks = unit_rows.astype(jnp.float32).reshape(NBLK, BLK, D)
    flat_pairs = pair_list.reshape(NDEV * CAP, 2).astype(jnp.int32)
    live_slots = (jnp.arange(CAP, dtype=jnp.int32)[None, :] < pair_count.astype(jnp.int32)[:, None]).reshape(NDEV * CAP)
    diagonal = jnp.eye(BLK, dtype=bool)

    def visit(best_rows, pair_item):
        pair_ids, active = pair_item

        def update(best_rows):
            left_block = blocks[pair_ids[0]]
            right_block = blocks[pair_ids[1]]
            similar = jnp.dot(left_block, right_block.T, precision=lax.Precision.HIGHEST)
            similar = jnp.where(diagonal & (pair_ids[0] == pair_ids[1]), lowest, similar)
            best_rows = best_rows.at[pair_ids[0]].max(lax.optimization_barrier(jnp.max(similar, axis=1)))
            best_rows = best_rows.at[pair_ids[1]].max(lax.optimization_barrier(jnp.max(similar, axis=0)))
            return best_rows
        return (lax.cond(active, update, lambda kept: kept, best_rows), None)
    start_rows = jnp.full((NBLK, BLK), lowest, jnp.float32)
    best_rows, _ = lax.scan(visit, start_rows, (flat_pairs, live_slots))
    return best_rows.reshape(NBLK * BLK)
```

```python
import functools
import itertools

import jax
import jax.numpy as jnp
from jax import lax
from jax.experimental import pallas as pl
from jax.experimental.pallas import tpu as pltpu
from jax.sharding import PartitionSpec as P

MESH = pl.DeviceIdType.MESH
BLK = 256
LANES = 128
SUBLANES = 8
lowest = -3.0
epsilon = 1e-06


class Plan:
    def __init__(self, chips):
        self.chips = chips
        if chips == 8:
            self.parts, self.steps = 1, 2
            self.moves = [
                [i ^ 1 for i in range(8)],
                [i + 2 if i < 6 else -1 for i in range(8)],
                [i - 2 if i > 1 else -1 for i in range(8)],
            ]
            second = [
                [2, 3, 4, 5, 2, 3, 4, 5],
                [1, 0, 3, 2, 2, 3, -1, -1],
                [-1, -1, 4, 5, 6, 7, 7, 6],
            ]
            self.sends = [
                [[(i, 0) if to[i] >= 0 else None for i in range(8)], [(u, 0) if u >= 0 else None for u in later]]
                for to, later in zip(self.moves, second)
            ]
        else:
            self.parts, self.steps = 1, chips // 2
            self.moves = [[(i + 1) % chips for i in range(chips)]]
            self.sends = [[[((i - t) % chips, 0) for i in range(chips)] for t in range(self.steps)]]
        self.slots = self.parts + len(self.moves) * self.steps
        self.unit_of = [[None] * self.slots for _ in range(chips)]
        self.held = [{} for _ in range(chips)]
        for i in range(chips):
            for h in range(self.parts):
                self.unit_of[i][h] = (i, h)
                self.held[i][(i, h)] = (0, h)
        self.source = [[[-1] * chips for _ in range(self.steps)] for _ in self.moves]
        for t in range(self.steps):
            arrived = []
            for d, to in enumerate(self.moves):
                for i in range(chips):
                    unit = self.sends[d][t][i]
                    if unit is None:
                        continue
                    self.source[d][t][i] = self.held[i][unit][1]
                    slot = self.parts + d * self.steps + t
                    self.unit_of[to[i]][slot] = unit
                    arrived.append((to[i], unit, slot))
            for i, unit, slot in arrived:
                self.held[i].setdefault(unit, (t + 1, slot))
        self.assign()

    def assign(self):
        units = [(i, h) for i in range(self.chips) for h in range(self.parts)]
        options = []
        for a, b in itertools.combinations_with_replacement(units, 2):
            places = []
            for i in range(self.chips):
                if a in self.held[i] and b in self.held[i]:
                    places.append((max(self.held[i][a][0], self.held[i][b][0]), i))
            assert places
            first = min(places)[0]
            places = [i for stage, i in places if stage == first]
            options.append((len(places), first, a, b, places))
        options.sort()
        load = [[0] * self.chips for _ in range(self.steps + 1)]
        chosen = []
        for _, stage, a, b, places in options:
            i = min(places, key=lambda k: (load[stage][k], k))
            load[stage][i] += 1
            chosen.append([stage, a, b, places, i])
        moved = True
        while moved:
            moved = False
            for item in chosen:
                stage, a, b, places, i = item
                for k in places:
                    if load[stage][k] + 1 < load[stage][i]:
                        load[stage][k] += 1
                        load[stage][i] -= 1
                        item[4] = i = k
                        moved = True
        self.work = [[[] for _ in range(self.chips)] for _ in range(self.steps + 1)]
        for stage, a, b, _, i in chosen:
            one, two = self.held[i][a], self.held[i][b]
            u, v = (one, two) if one[0] >= two[0] else (two, one)
            self.work[stage][i].append((u[1], v[1]))
        for stage in self.work:
            longest = max(len(pairs) for pairs in stage)
            for pairs in stage:
                while len(pairs) < longest:
                    pairs.append(pairs[-1] if pairs else (0, 0))


def pick(values, index):
    if all(v == values[0] for v in values):
        return jnp.int32(values[0])
    result = jnp.int32(values[-1])
    for i in range(len(values) - 1):
        result = jnp.where(index == i, jnp.int32(values[i]), result)
    return result


def kernel(
    plan, cols, x_ref, o_ref, buf, row_acc, col_acc, parts, got,
    send_sem, recv_sem, side_send, side_recv, part_send, part_recv,
):
    me, core = lax.axis_index("rows"), lax.axis_index("cols")
    chips, steps, own = plan.chips, plan.steps, plan.parts
    rows, width = x_ref.shape
    unit = rows // own
    others = [(k, q) for k in range(chips) for q in range(cols) if (k, q) != (0, 0)]

    def device(k, q):
        return {"rows": lax.rem(me + k, chips), "cols": lax.rem(core + q, cols)}

    barrier = pltpu.get_barrier_semaphore()
    for k, q in others:
        pl.semaphore_signal(barrier, inc=1, device_id=device(k, q), device_id_type=MESH)

    for h in range(own):
        values = x_ref[h * unit:(h + 1) * unit, :].astype(jnp.float32)
        mean = jnp.mean(values * values, axis=1, keepdims=True)
        buf[h, 0] = (values * lax.rsqrt(mean + epsilon) * width ** (-0.5)).astype(jnp.bfloat16)

    pl.semaphore_wait(barrier, len(others))

    def present(table, index):
        return pick([int(v >= 0) for v in table], index) == 1

    def guarded(table, index, action):
        if all(v >= 0 for v in table):
            action()
        elif any(v >= 0 for v in table):
            pl.when(present(table, index))(action)

    def link_copy(d, t):
        slot = own + d * steps + t
        return pltpu.make_async_remote_copy(
            src_ref=buf.at[pick([max(v, 0) for v in plan.source[d][t]], me), 0],
            dst_ref=buf.at[slot, 0],
            send_sem=send_sem.at[d, t],
            recv_sem=recv_sem.at[d, t],
            device_id={"rows": pick([max(v, 0) for v in plan.moves[d]], me), "cols": core},
            device_id_type=MESH,
        )

    def incoming(d, t):
        result = [-1] * chips
        for i in range(chips):
            if plan.source[d][t][i] >= 0:
                result[plan.moves[d][i]] = 1
        return result

    def side_copy(slot, q):
        return pltpu.make_async_remote_copy(
            src_ref=buf.at[slot, 0],
            dst_ref=buf.at[slot, (cols - q) % cols],
            send_sem=side_send.at[slot, q],
            recv_sem=side_recv.at[slot, (cols - q) % cols],
            device_id=device(0, q),
            device_id_type=MESH,
        )

    def start_sends(t):
        for d in range(len(plan.moves)):
            guarded(plan.source[d][t], me, lambda: link_copy(d, t).start())

    def tile(u, v, q, col0, same):
        left = buf[u, 0]
        right = buf[v, q, pl.ds(col0, BLK), :]
        similar = lax.dot_general(
            left, right, (((1,), (1,)), ((), ())), preferred_element_type=jnp.float32
        )
        row_ids = lax.broadcasted_iota(jnp.int32, similar.shape, 0)
        col_ids = lax.broadcasted_iota(jnp.int32, similar.shape, 1) + col0
        limit = jnp.where(same, 0, rows)
        similar = jnp.where(row_ids == col_ids + limit, lowest, similar)
        best = row_acc[u]
        for j in range(BLK // LANES):
            best = jnp.maximum(best, similar[:, j * LANES:(j + 1) * LANES])
        row_acc[u] = best
        tall = jnp.max(similar.reshape(unit // SUBLANES, SUBLANES, BLK), axis=0)
        col_acc[v, q, :, pl.ds(col0, BLK)] = jnp.maximum(col_acc[v, q, :, pl.ds(col0, BLK)], tall)

    def multiply(stage):
        lists = plan.work[stage]
        count = len(lists[0])
        if not count:
            return
        bits = max(plan.slots - 1, 1).bit_length()
        per_word = 30 // (2 * bits)
        words = []
        for first in range(0, count, per_word):
            packed = []
            for i in range(chips):
                word = 0
                for n, (u, v) in enumerate(lists[i][first:first + per_word]):
                    word |= (u | v << bits) << (2 * bits * n)
                packed.append(word)
            words.append(pick(packed, me))
        tiles = unit // BLK

        @pl.loop(0, count * cols * tiles)
        def _(step):
            p, rest = step // (cols * tiles), step % (cols * tiles)
            q, j = rest // tiles, rest % tiles
            word = words[0]
            for n in range(1, len(words)):
                word = jnp.where(p >= n * per_word, words[n], word)
            word = word >> (2 * bits * (p % per_word))
            u, v = word & (2 ** bits - 1), (word >> bits) & (2 ** bits - 1)
            tile(u, v, q, pl.multiple_of(j * BLK, BLK), (u == v) & (q == 0))

    start_sends(0)
    for h in range(own):
        for q in range(1, cols):
            side_copy(h, q).start()
    row_acc[...] = jnp.full(row_acc.shape, lowest, jnp.float32)
    col_acc[...] = jnp.full(col_acc.shape, lowest, jnp.float32)
    parts[...] = jnp.full(parts.shape, lowest, jnp.float32)
    for h in range(own):
        for q in range(1, cols):
            side_copy(h, q).wait_recv()
    multiply(0)
    for t in range(steps):
        for d in range(len(plan.moves)):
            guarded(incoming(d, t), me, lambda: link_copy(d, t).wait_recv())
        if t + 1 < steps:
            start_sends(t + 1)
        for d in range(len(plan.moves)):
            for q in range(1, cols):
                guarded(incoming(d, t), me, lambda: side_copy(own + d * steps + t, q).start())
        for d in range(len(plan.moves)):
            for q in range(1, cols):
                guarded(incoming(d, t), me, lambda: side_copy(own + d * steps + t, q).wait_recv())
        multiply(t + 1)

    for slot in range(plan.slots):
        names = [plan.unit_of[i][slot] for i in range(chips)]
        chip_table = [name[0] if name else -1 for name in names]
        part_table = [name[1] if name else 0 for name in names]

        def fold():
            chip, part = pick([max(v, 0) for v in chip_table], me), pick(part_table, me)
            across = jnp.max(jnp.transpose(row_acc[slot]), axis=0, keepdims=True)
            for q in range(cols):
                best = jnp.max(col_acc[slot, q], axis=0, keepdims=True)
                if q == 0:
                    best = jnp.maximum(best, across)
                place = chip * cols + q
                parts[place, part] = jnp.maximum(parts[place, part], best)

        guarded(chip_table, me, fold)

    def part_copy(k, q):
        return pltpu.make_async_remote_copy(
            src_ref=parts.at[lax.rem(me + k, chips) * cols + q],
            dst_ref=got.at[k * cols + q],
            send_sem=part_send.at[k * cols + q],
            recv_sem=part_recv.at[k * cols + q],
            device_id=device(k, q),
            device_id_type=MESH,
        )

    for k, q in others:
        part_copy(k, q).start()
    result = parts[me * cols]
    for k, q in others:
        part_copy(k, q).wait_recv()
    for k, q in others:
        result = jnp.maximum(result, got[k * cols + q])
    for h in range(own):
        o_ref[:, h * unit:(h + 1) * unit] = result[h]

    for k, q in others:
        part_copy(k, q).wait_send()
    for t in range(steps):
        for d in range(len(plan.moves)):
            guarded(plan.source[d][t], me, lambda: link_copy(d, t).wait_send())
            for q in range(1, cols):
                guarded(incoming(d, t), me, lambda: side_copy(own + d * steps + t, q).wait_send())
    for h in range(own):
        for q in range(1, cols):
            side_copy(h, q).wait_send()


def shards(embeddings, pair_list, pair_count):
    chips, cols = lax.axis_size("rows"), lax.axis_size("cols")
    rows, width = embeddings.shape
    plan = Plan(chips)
    unit = rows // plan.parts
    total = chips * cols
    best = pl.pallas_call(
        functools.partial(kernel, plan, cols),
        out_shape=jax.ShapeDtypeStruct((1, rows), jnp.float32),
        in_specs=[pl.BlockSpec(memory_space=pltpu.VMEM)],
        out_specs=pl.BlockSpec(memory_space=pltpu.VMEM),
        scratch_shapes=[
            pltpu.VMEM((plan.slots, cols, unit, width), jnp.bfloat16),
            pltpu.VMEM((plan.slots, unit, LANES), jnp.float32),
            pltpu.VMEM((plan.slots, cols, SUBLANES, unit), jnp.float32),
            pltpu.VMEM((total, plan.parts, 1, unit), jnp.float32),
            pltpu.VMEM((total, plan.parts, 1, unit), jnp.float32),
            pltpu.SemaphoreType.DMA((len(plan.moves), plan.steps)),
            pltpu.SemaphoreType.DMA((len(plan.moves), plan.steps)),
            pltpu.SemaphoreType.DMA((plan.slots, cols)),
            pltpu.SemaphoreType.DMA((plan.slots, cols)),
            pltpu.SemaphoreType.DMA((total,)),
            pltpu.SemaphoreType.DMA((total,)),
        ],
        compiler_params=pltpu.CompilerParams(
            collective_id=0, has_side_effects=True, vmem_limit_bytes=48 * 2 ** 20
        ),
    )(embeddings)
    return best.reshape(rows)


def solution(mesh):
    in_specs = (
        P(("groups", "rows", "cols"), None),
        P(("rows", "cols"), None, None),
        P(("rows", "cols")),
    )
    out_specs = P(("groups", "rows", "cols"))
    return jax.shard_map(shards, mesh=mesh, in_specs=in_specs, out_specs=out_specs, check_vma=False)
```

```python
import functools
import itertools

import jax
import jax.numpy as jnp
from jax import lax
from jax.experimental import pallas as pl
from jax.experimental.pallas import tpu as pltpu
from jax.sharding import PartitionSpec as P

MESH = pl.DeviceIdType.MESH
BLK = 256
LANES = 128
SUBLANES = 8
lowest = -3.0
epsilon = 1e-06


class Plan:
    def __init__(self, chips):
        self.chips = chips
        self.parts, self.steps = 1, chips // 2
        self.moves = [[(i + 1) % chips for i in range(chips)]]
        self.sends = [[[((i - t) % chips, 0) for i in range(chips)] for t in range(self.steps)]]
        self.slots = self.parts + len(self.moves) * self.steps
        self.unit_of = [[None] * self.slots for _ in range(chips)]
        self.held = [{} for _ in range(chips)]
        for i in range(chips):
            for h in range(self.parts):
                self.unit_of[i][h] = (i, h)
                self.held[i][(i, h)] = (0, h)
        self.source = [[[-1] * chips for _ in range(self.steps)] for _ in self.moves]
        for t in range(self.steps):
            arrived = []
            for d, to in enumerate(self.moves):
                for i in range(chips):
                    unit = self.sends[d][t][i]
                    if unit is None:
                        continue
                    self.source[d][t][i] = self.held[i][unit][1]
                    slot = self.parts + d * self.steps + t
                    self.unit_of[to[i]][slot] = unit
                    arrived.append((to[i], unit, slot))
            for i, unit, slot in arrived:
                self.held[i].setdefault(unit, (t + 1, slot))
        self.assign()

    def assign(self):
        units = [(i, h) for i in range(self.chips) for h in range(self.parts)]
        options = []
        for a, b in itertools.combinations_with_replacement(units, 2):
            places = []
            for i in range(self.chips):
                if a in self.held[i] and b in self.held[i]:
                    places.append((max(self.held[i][a][0], self.held[i][b][0]), i))
            assert places
            first = min(places)[0]
            places = [i for stage, i in places if stage == first]
            options.append((len(places), first, a, b, places))
        options.sort()
        load = [[0] * self.chips for _ in range(self.steps + 1)]
        chosen = []
        for _, stage, a, b, places in options:
            i = min(places, key=lambda k: (load[stage][k], k))
            load[stage][i] += 1
            chosen.append([stage, a, b, places, i])
        moved = True
        while moved:
            moved = False
            for item in chosen:
                stage, a, b, places, i = item
                for k in places:
                    if load[stage][k] + 1 < load[stage][i]:
                        load[stage][k] += 1
                        load[stage][i] -= 1
                        item[4] = i = k
                        moved = True
        self.work = [[[] for _ in range(self.chips)] for _ in range(self.steps + 1)]
        for stage, a, b, _, i in chosen:
            one, two = self.held[i][a], self.held[i][b]
            u, v = (one, two) if one[0] >= two[0] else (two, one)
            self.work[stage][i].append((u[1], v[1]))
        for stage in self.work:
            longest = max(len(pairs) for pairs in stage)
            for pairs in stage:
                while len(pairs) < longest:
                    pairs.append(pairs[-1] if pairs else (0, 0))


def pick(values, index):
    if all(v == values[0] for v in values):
        return jnp.int32(values[0])
    result = jnp.int32(values[-1])
    for i in range(len(values) - 1):
        result = jnp.where(index == i, jnp.int32(values[i]), result)
    return result


def kernel(
    plan, cols, x_ref, o_ref, buf, row_acc, col_acc, parts, got,
    send_sem, recv_sem, side_send, side_recv, part_send, part_recv,
):
    me, core = lax.axis_index("rows"), lax.axis_index("cols")
    chips, steps, own = plan.chips, plan.steps, plan.parts
    rows, width = x_ref.shape
    unit = rows // own
    others = [(k, q) for k in range(chips) for q in range(cols) if (k, q) != (0, 0)]

    def device(k, q):
        return {"rows": lax.rem(me + k, chips), "cols": lax.rem(core + q, cols)}

    barrier = pltpu.get_barrier_semaphore()
    for k, q in others:
        pl.semaphore_signal(barrier, inc=1, device_id=device(k, q), device_id_type=MESH)

    for h in range(own):
        values = x_ref[h * unit:(h + 1) * unit, :].astype(jnp.float32)
        mean = jnp.mean(values * values, axis=1, keepdims=True)
        buf[h, 0] = (values * lax.rsqrt(mean + epsilon) * width ** (-0.5)).astype(jnp.bfloat16)

    pl.semaphore_wait(barrier, len(others))

    def present(table, index):
        return pick([int(v >= 0) for v in table], index) == 1

    def guarded(table, index, action):
        if all(v >= 0 for v in table):
            action()
        elif any(v >= 0 for v in table):
            pl.when(present(table, index))(action)

    def link_copy(d, t):
        slot = own + d * steps + t
        return pltpu.make_async_remote_copy(
            src_ref=buf.at[pick([max(v, 0) for v in plan.source[d][t]], me), 0],
            dst_ref=buf.at[slot, 0],
            send_sem=send_sem.at[d, t],
            recv_sem=recv_sem.at[d, t],
            device_id={"rows": pick([max(v, 0) for v in plan.moves[d]], me), "cols": core},
            device_id_type=MESH,
        )

    def incoming(d, t):
        result = [-1] * chips
        for i in range(chips):
            if plan.source[d][t][i] >= 0:
                result[plan.moves[d][i]] = 1
        return result

    def side_copy(slot, q):
        return pltpu.make_async_remote_copy(
            src_ref=buf.at[slot, 0],
            dst_ref=buf.at[slot, (cols - q) % cols],
            send_sem=side_send.at[slot, q],
            recv_sem=side_recv.at[slot, (cols - q) % cols],
            device_id=device(0, q),
            device_id_type=MESH,
        )

    def start_sends(t):
        for d in range(len(plan.moves)):
            guarded(plan.source[d][t], me, lambda: link_copy(d, t).start())

    def tile(u, v, q, col0, same):
        left = buf[u, 0]
        right = buf[v, q, pl.ds(col0, BLK), :]
        similar = lax.dot_general(
            left, right, (((1,), (1,)), ((), ())), preferred_element_type=jnp.float32
        )
        row_ids = lax.broadcasted_iota(jnp.int32, similar.shape, 0)
        col_ids = lax.broadcasted_iota(jnp.int32, similar.shape, 1) + col0
        limit = jnp.where(same, 0, rows)
        similar = jnp.where(row_ids == col_ids + limit, lowest, similar)
        best = row_acc[u]
        for j in range(BLK // LANES):
            best = jnp.maximum(best, similar[:, j * LANES:(j + 1) * LANES])
        row_acc[u] = best
        tall = jnp.max(similar.reshape(unit // SUBLANES, SUBLANES, BLK), axis=0)
        col_acc[v, q, :, pl.ds(col0, BLK)] = jnp.maximum(col_acc[v, q, :, pl.ds(col0, BLK)], tall)

    def multiply(stage):
        lists = plan.work[stage]
        count = len(lists[0])
        if not count:
            return
        bits = max(plan.slots - 1, 1).bit_length()
        per_word = 30 // (2 * bits)
        words = []
        for first in range(0, count, per_word):
            packed = []
            for i in range(chips):
                word = 0
                for n, (u, v) in enumerate(lists[i][first:first + per_word]):
                    word |= (u | v << bits) << (2 * bits * n)
                packed.append(word)
            words.append(pick(packed, me))
        tiles = unit // BLK

        @pl.loop(0, count * cols * tiles)
        def _(step):
            p, rest = step // (cols * tiles), step % (cols * tiles)
            q, j = rest // tiles, rest % tiles
            word = words[0]
            for n in range(1, len(words)):
                word = jnp.where(p >= n * per_word, words[n], word)
            word = word >> (2 * bits * (p % per_word))
            u, v = word & (2 ** bits - 1), (word >> bits) & (2 ** bits - 1)
            tile(u, v, q, pl.multiple_of(j * BLK, BLK), (u == v) & (q == 0))

    start_sends(0)
    for h in range(own):
        for q in range(1, cols):
            side_copy(h, q).start()
    row_acc[...] = jnp.full(row_acc.shape, lowest, jnp.float32)
    col_acc[...] = jnp.full(col_acc.shape, lowest, jnp.float32)
    parts[...] = jnp.full(parts.shape, lowest, jnp.float32)
    for h in range(own):
        for q in range(1, cols):
            side_copy(h, q).wait_recv()
    multiply(0)
    for t in range(steps):
        for d in range(len(plan.moves)):
            guarded(incoming(d, t), me, lambda: link_copy(d, t).wait_recv())
        if t + 1 < steps:
            start_sends(t + 1)
        for d in range(len(plan.moves)):
            for q in range(1, cols):
                guarded(incoming(d, t), me, lambda: side_copy(own + d * steps + t, q).start())
        for d in range(len(plan.moves)):
            for q in range(1, cols):
                guarded(incoming(d, t), me, lambda: side_copy(own + d * steps + t, q).wait_recv())
        multiply(t + 1)

    for slot in range(plan.slots):
        names = [plan.unit_of[i][slot] for i in range(chips)]
        chip_table = [name[0] if name else -1 for name in names]
        part_table = [name[1] if name else 0 for name in names]

        def fold():
            chip, part = pick([max(v, 0) for v in chip_table], me), pick(part_table, me)
            across = jnp.max(jnp.transpose(row_acc[slot]), axis=0, keepdims=True)
            for q in range(cols):
                best = jnp.max(col_acc[slot, q], axis=0, keepdims=True)
                if q == 0:
                    best = jnp.maximum(best, across)
                place = chip * cols + q
                parts[place, part] = jnp.maximum(parts[place, part], best)

        guarded(chip_table, me, fold)

    def part_copy(k, q):
        return pltpu.make_async_remote_copy(
            src_ref=parts.at[lax.rem(me + k, chips) * cols + q],
            dst_ref=got.at[k * cols + q],
            send_sem=part_send.at[k * cols + q],
            recv_sem=part_recv.at[k * cols + q],
            device_id=device(k, q),
            device_id_type=MESH,
        )

    for k, q in others:
        part_copy(k, q).start()
    result = parts[me * cols]
    for k, q in others:
        part_copy(k, q).wait_recv()
    for k, q in others:
        result = jnp.maximum(result, got[k * cols + q])
    for h in range(own):
        o_ref[:, h * unit:(h + 1) * unit] = result[h]

    for k, q in others:
        part_copy(k, q).wait_send()
    for t in range(steps):
        for d in range(len(plan.moves)):
            guarded(plan.source[d][t], me, lambda: link_copy(d, t).wait_send())
            for q in range(1, cols):
                guarded(incoming(d, t), me, lambda: side_copy(own + d * steps + t, q).wait_send())
    for h in range(own):
        for q in range(1, cols):
            side_copy(h, q).wait_send()


OWN, YNB, LOW, FAR, TOP, PASS, BACK = range(7)
CHUNKS = 8
PIECE = 128
ALL, FIRST, SECOND = range(CHUNKS), range(CHUNKS // 2), range(CHUNKS // 2, CHUNKS)
A_ORDER = list(SECOND) + list(FIRST)
ROUTES = {
    (0, OWN): [("x", PASS, A_ORDER), ("u", LOW, ALL), ("y", YNB, ALL)],
    (1, OWN): [("u", LOW, ALL), ("y", YNB, ALL)],
    (2, OWN): [("y", YNB, ALL)],
    (3, OWN): [("x", BACK, SECOND), ("d", TOP, FIRST), ("y", YNB, ALL)],
    (3, PASS): [("d", PASS, ALL)],
    (2, PASS): [("d", PASS, ALL)],
    (1, PASS): [("x", FAR, ALL), ("d", PASS, SECOND)],
    (0, PASS): [("x", FAR, SECOND)],
    (0, BACK): [("u", BACK, SECOND)],
    (1, BACK): [("x", TOP, SECOND)],
    (2, LOW): [("u", LOW, ALL)],
    (2, FAR): [("u", FAR, FIRST)],
}
OWNER = {OWN: [0, 1, 2, 3], YNB: [0, 1, 2, 3], LOW: [-1, 0, 1, 1], FAR: [-1, -1, 0, 0], TOP: [-1, -1, 3, -1]}
BUDGET = 6


def target(place, way):
    return {"x": 3 - place, "y": place, "u": place + 1, "d": place - 1}[way]


def relay_plan():
    def depth(place, slot, chunk):
        return max(
            [1 + depth(target(place, way), to, chunk) for way, to, which in ROUTES.get((place, slot), []) if chunk in which],
            default=0,
        )

    queues = {}

    def enqueue(place, slot, chunk, step, order):
        for way, to, which in ROUTES.get((place, slot), []):
            if chunk in which:
                rank = -1 - depth(target(place, way), to, chunk)
                place_in = list(which).index(chunk) if slot == OWN else order
                queues.setdefault((place, way), []).append((rank, place_in, slot, to, chunk, step))

    arrived = {(p, OWN, c): 0 for p in range(4) for c in ALL}
    for p in range(4):
        for c in ALL:
            enqueue(p, OWN, c, 0, c)
    waits, sends, step = [], [], 0
    landing = []
    while landing or any(queues.values()):
        waits.append([[] for _ in range(4)])
        sends.append([[] for _ in range(4)])
        for p, slot, c in landing:
            arrived[p, slot, c] = step
            waits[step][p].append((slot, c))
            enqueue(p, slot, c, step, step)
        landing = []
        for (p, way), queue in queues.items():
            if queue:
                item = min(queue)
                queue.remove(item)
                _, _, slot, to, c, ready = item
                sends[max(ready, step - 1)][p].append((way, slot, to, c))
                landing.append((target(p, way), to, c))
        step += 1
    steps = len(waits)
    share = max(arrived[p, YNB, c] for p in range(4) for c in ALL)
    work = [[[] for _ in range(4)] for _ in range(steps + 1)]
    for p in range(4):
        jobs = []
        pieces = range(2)

        def ready(slot, piece):
            per = CHUNKS // PIECES
            return max(arrived[p, slot, c] for c in range(piece * per, piece * per + per))

        for piece in range(PIECES):
            jobs += [(1, (OWN, piece, OWN, q)) for q in range(2)]
            jobs.append((share + 1, (OWN, piece, YNB, 2)))
            for slot in (LOW, FAR, TOP):
                if OWNER[slot][p] >= 0:
                    at = ready(slot, piece)
                    jobs += [(max(1, at), (slot, piece, OWN, q)) for q in range(2)]
                    jobs += [(max(share + 1, at), (slot, piece, YNB, q)) for q in range(2)]
        if p == 0:
            jobs = [j for j in jobs]
        jobs.sort()
        for t in range(steps + 1):
            able = [j for j in jobs if j[0] <= t]
            take = able if t == steps else able[:BUDGET]
            work[t][p] = [j[1] for j in take]
            jobs = [j for j in jobs if j not in take]
        assert not jobs
    return waits, sends, work, share


PIECES = 512 // PIECE


def relay_kernel(
    x_ref, o_ref, buf, row_acc, col_acc, parts, got,
    send_sem, recv_sem, side_send, side_recv, part_send, part_recv,
):
    waits, sends, work, share = relay_plan()
    group, line, core = lax.axis_index("groups"), lax.axis_index("rows"), lax.axis_index("cols")
    z, y = line // 2, line % 2
    place = z + group * (3 - 2 * z)
    rows, width = x_ref.shape
    chunk_rows = rows // CHUNKS
    upward = 1 - 2 * group

    def neighbour(way):
        if way == "x":
            return {"groups": 1 - group, "rows": line, "cols": core}
        if way == "y":
            return {"groups": group, "rows": 2 * z + 1 - y, "cols": core}
        step = upward if way == "u" else -upward
        return {"groups": group, "rows": line + 2 * step, "cols": core}

    def device_at(at, dy, q):
        zz = at + group * (3 - 2 * at)
        return {"groups": group, "rows": 2 * zz + (y + dy) % 2, "cols": (core + q) % 2}

    barrier = pltpu.get_barrier_semaphore()
    everyone = [(k, q) for k in range(8) for q in range(2) if (k, q) != (0, 0)]
    pl.semaphore_signal(barrier, inc=1, device_id=neighbour("x"), device_id_type=MESH)
    for k, q in everyone:
        other = {"groups": group, "rows": (line + k) % 8, "cols": (core + q) % 2}
        pl.semaphore_signal(barrier, inc=1, device_id=other, device_id_type=MESH)

    @pl.loop(0, CHUNKS)
    def _(c):
        at = pl.ds(pl.multiple_of(c * chunk_rows, chunk_rows), chunk_rows)
        values = x_ref[at, :].astype(jnp.float32)
        mean = jnp.mean(values * values, axis=1, keepdims=True)
        buf[OWN, 0, at, :] = (values * lax.rsqrt(mean + epsilon) * width ** (-0.5)).astype(jnp.bfloat16)

    pl.semaphore_wait(barrier, len(everyone) + 1)

    def link_copy(way, slot, to, c, n):
        at = pl.ds(c * chunk_rows, chunk_rows)
        return pltpu.make_async_remote_copy(
            src_ref=buf.at[slot, 0, at],
            dst_ref=buf.at[to, 0, at],
            send_sem=send_sem.at[n],
            recv_sem=recv_sem.at[to, c],
            device_id=neighbour(way),
            device_id_type=MESH,
        )

    def arrival(slot, c):
        return link_copy("x", slot, slot, c, 0)

    def side_copy(n):
        slot = OWN if n == 0 else YNB
        return pltpu.make_async_remote_copy(
            src_ref=buf.at[slot, 0],
            dst_ref=buf.at[slot, 1],
            send_sem=side_send.at[n],
            recv_sem=side_recv.at[n],
            device_id={"groups": group, "rows": line, "cols": 1 - core},
            device_id_type=MESH,
        )

    def multiply(lists):
        longest = max(len(items) for items in lists)
        if not longest:
            return
        packed = [
            [sum((u | piece << 3 | v << 6 | q << 7) << (9 * i) for i, (u, piece, v, q) in enumerate(items[n:n + 3]))
             for items in lists]
            for n in range(0, longest, 3)
        ]
        words = [pick(entry, place) for entry in packed]

        @pl.loop(0, pick([len(items) for items in lists], place))
        def _(n):
            word = words[0]
            for k in range(1, len(words)):
                word = jnp.where(n >= 3 * k, words[k], word)
            word = word >> (9 * (n % 3))
            u, piece, v, q = word & 7, (word >> 3) & 7, (word >> 6) & 1, (word >> 7) & 3
            q = jnp.where(q == 2, y, q)
            at = pl.ds(pl.multiple_of(piece * PIECE, PIECE), PIECE)
            similar = lax.dot_general(
                buf[u, 0, at, :], buf[v, q], (((1,), (1,)), ((), ())), preferred_element_type=jnp.float32
            )
            shift = jnp.where((u == OWN) & (v == OWN) & (q == 0), piece * PIECE, 2 * rows)
            row_ids = lax.broadcasted_iota(jnp.int32, similar.shape, 0)
            col_ids = lax.broadcasted_iota(jnp.int32, similar.shape, 1)
            similar = jnp.where(col_ids - row_ids == shift, lowest, similar)
            best = row_acc[u, at]
            for j in range(rows // LANES):
                best = jnp.maximum(best, similar[:, j * LANES:(j + 1) * LANES])
            row_acc[u, at] = best
            tall = jnp.max(similar.reshape(PIECE // SUBLANES, SUBLANES, rows), axis=0)
            col_acc[v, q] = jnp.maximum(col_acc[v, q], tall)

    steps = len(waits)
    numbers = [0] * 4
    started = [[] for _ in range(4)]
    for t in range(steps):
        if t == 1:
            side_copy(0).wait_recv()
        if t == share + 1:
            side_copy(1).wait_recv()
        for p in range(4):

            @pl.when(place == p)
            def _():
                early = [s for s in sends[t][p] if (s[1], s[3]) not in waits[t][p]]
                for send in early:
                    link_copy(*send, numbers[p]).start()
                    started[p].append((*send, numbers[p]))
                    numbers[p] += 1
                for slot, c in waits[t][p]:
                    arrival(slot, c).wait_recv()
                    for send in sends[t][p]:
                        if (send[1], send[3]) == (slot, c):
                            link_copy(*send, numbers[p]).start()
                            started[p].append((*send, numbers[p]))
                            numbers[p] += 1

        if t == 0:
            side_copy(0).start()
            row_acc[...] = jnp.full(row_acc.shape, lowest, jnp.float32)
            col_acc[...] = jnp.full(col_acc.shape, lowest, jnp.float32)
        if t == share:
            side_copy(1).start()
        multiply(work[t])
    multiply(work[steps])

    for slot in range(TOP + 1):

        def fold(slot=slot):
            across = jnp.max(jnp.transpose(row_acc[slot]), axis=0, keepdims=True)
            if slot <= YNB:
                down = [jnp.max(col_acc[slot, q], axis=0, keepdims=True) for q in range(2)]
                parts[slot, 0] = jnp.maximum(across, down[0])
                parts[slot, 1] = down[1]
            else:
                parts[slot, 0] = across

        if min(OWNER[slot]) >= 0:
            fold()
        else:
            pl.when(present(OWNER[slot], place))(fold)

    def part_copy(slot, p, q):
        n = 2 * slot + q
        dy = 1 if slot == YNB else 0
        return pltpu.make_async_remote_copy(
            src_ref=parts.at[slot, q],
            dst_ref=got.at[p, dy, q],
            send_sem=part_send.at[n],
            recv_sem=part_recv.at[p, dy, q],
            device_id=device_at(OWNER[slot][p], dy, q),
            device_id_type=MESH,
        )

    def messages(p):
        result = [(OWN, 1), (YNB, 0), (YNB, 1)]
        return result + [(slot, 0) for slot in (LOW, FAR, TOP) if OWNER[slot][p] >= 0]

    for p in range(4):

        @pl.when(place == p)
        def _():
            for slot, q in messages(p):
                part_copy(slot, p, q).start()

    o_ref[...] = parts[OWN, 0]
    for p in range(4):

        @pl.when(place == p)
        def _():
            sources = []
            for sender in range(4):
                for slot, q in messages(sender):
                    if OWNER[slot][sender] == p:
                        sources.append((sender, 1 if slot == YNB else 0, q))
                        part_copy(slot, sender, q).wait_recv()
            best = o_ref[...]
            for source in sources:
                best = jnp.maximum(best, got[source])
            o_ref[...] = best
            for slot, q in messages(p):
                part_copy(slot, p, q).wait_send()
            for way, slot, to, c, n in started[p]:
                link_copy(way, slot, to, c, n).wait_send()

    for n in range(2):
        side_copy(n).wait_send()


def present(table, index):
    return pick([int(v >= 0) for v in table], index) == 1


def relayed(embeddings):
    rows, width = embeddings.shape
    best = pl.pallas_call(
        relay_kernel,
        out_shape=jax.ShapeDtypeStruct((1, rows), jnp.float32),
        in_specs=[pl.BlockSpec(memory_space=pltpu.VMEM)],
        out_specs=pl.BlockSpec(memory_space=pltpu.VMEM),
        scratch_shapes=[
            pltpu.VMEM((BACK + 1, 2, rows, width), jnp.bfloat16),
            pltpu.VMEM((TOP + 1, rows, LANES), jnp.float32),
            pltpu.VMEM((2, 2, SUBLANES, rows), jnp.float32),
            pltpu.VMEM((TOP + 1, 2, 1, rows), jnp.float32),
            pltpu.VMEM((4, 2, 2, 1, rows), jnp.float32),
            pltpu.SemaphoreType.DMA((64,)),
            pltpu.SemaphoreType.DMA((BACK + 1, CHUNKS)),
            pltpu.SemaphoreType.DMA((2,)),
            pltpu.SemaphoreType.DMA((2,)),
            pltpu.SemaphoreType.DMA((2 * TOP + 2,)),
            pltpu.SemaphoreType.DMA((4, 2, 2)),
        ],
        compiler_params=pltpu.CompilerParams(
            collective_id=1, has_side_effects=True, vmem_limit_bytes=48 * 2 ** 20
        ),
    )(embeddings)
    return best.reshape(rows)


def shards(embeddings, pair_list, pair_count):
    chips, cols = lax.axis_size("rows"), lax.axis_size("cols")
    rows, width = embeddings.shape
    if (lax.axis_size("groups"), chips, cols) == (2, 8, 2):
        return relayed(embeddings)
    plan = Plan(chips)
    unit = rows // plan.parts
    total = chips * cols
    best = pl.pallas_call(
        functools.partial(kernel, plan, cols),
        out_shape=jax.ShapeDtypeStruct((1, rows), jnp.float32),
        in_specs=[pl.BlockSpec(memory_space=pltpu.VMEM)],
        out_specs=pl.BlockSpec(memory_space=pltpu.VMEM),
        scratch_shapes=[
            pltpu.VMEM((plan.slots, cols, unit, width), jnp.bfloat16),
            pltpu.VMEM((plan.slots, unit, LANES), jnp.float32),
            pltpu.VMEM((plan.slots, cols, SUBLANES, unit), jnp.float32),
            pltpu.VMEM((total, plan.parts, 1, unit), jnp.float32),
            pltpu.VMEM((total, plan.parts, 1, unit), jnp.float32),
            pltpu.SemaphoreType.DMA((len(plan.moves), plan.steps)),
            pltpu.SemaphoreType.DMA((len(plan.moves), plan.steps)),
            pltpu.SemaphoreType.DMA((plan.slots, cols)),
            pltpu.SemaphoreType.DMA((plan.slots, cols)),
            pltpu.SemaphoreType.DMA((total,)),
            pltpu.SemaphoreType.DMA((total,)),
        ],
        compiler_params=pltpu.CompilerParams(
            collective_id=0, has_side_effects=True, vmem_limit_bytes=48 * 2 ** 20
        ),
    )(embeddings)
    return best.reshape(rows)


def solution(mesh):
    in_specs = (
        P(("groups", "rows", "cols"), None),
        P(("rows", "cols"), None, None),
        P(("rows", "cols")),
    )
    out_specs = P(("groups", "rows", "cols"))
    return jax.shard_map(shards, mesh=mesh, in_specs=in_specs, out_specs=out_specs, check_vma=False)
```

```python
import functools
import itertools

import jax
import jax.numpy as jnp
from jax import lax
from jax.experimental import pallas as pl
from jax.experimental.pallas import tpu as pltpu
from jax.sharding import PartitionSpec as P

MESH = pl.DeviceIdType.MESH
BLK = 256
LANES = 128
SUBLANES = 8
lowest = -3.0
epsilon = 1e-06


class Plan:
    def __init__(self, chips):
        self.chips = chips
        self.parts, self.steps = 1, chips // 2
        self.moves = [[(i + 1) % chips for i in range(chips)]]
        self.sends = [[[((i - t) % chips, 0) for i in range(chips)] for t in range(self.steps)]]
        self.slots = self.parts + len(self.moves) * self.steps
        self.unit_of = [[None] * self.slots for _ in range(chips)]
        self.held = [{} for _ in range(chips)]
        for i in range(chips):
            for h in range(self.parts):
                self.unit_of[i][h] = (i, h)
                self.held[i][(i, h)] = (0, h)
        self.source = [[[-1] * chips for _ in range(self.steps)] for _ in self.moves]
        for t in range(self.steps):
            arrived = []
            for d, to in enumerate(self.moves):
                for i in range(chips):
                    unit = self.sends[d][t][i]
                    if unit is None:
                        continue
                    self.source[d][t][i] = self.held[i][unit][1]
                    slot = self.parts + d * self.steps + t
                    self.unit_of[to[i]][slot] = unit
                    arrived.append((to[i], unit, slot))
            for i, unit, slot in arrived:
                self.held[i].setdefault(unit, (t + 1, slot))
        self.assign()

    def assign(self):
        units = [(i, h) for i in range(self.chips) for h in range(self.parts)]
        options = []
        for a, b in itertools.combinations_with_replacement(units, 2):
            places = []
            for i in range(self.chips):
                if a in self.held[i] and b in self.held[i]:
                    places.append((max(self.held[i][a][0], self.held[i][b][0]), i))
            assert places
            first = min(places)[0]
            places = [i for stage, i in places if stage == first]
            options.append((len(places), first, a, b, places))
        options.sort()
        load = [[0] * self.chips for _ in range(self.steps + 1)]
        chosen = []
        for _, stage, a, b, places in options:
            i = min(places, key=lambda k: (load[stage][k], k))
            load[stage][i] += 1
            chosen.append([stage, a, b, places, i])
        moved = True
        while moved:
            moved = False
            for item in chosen:
                stage, a, b, places, i = item
                for k in places:
                    if load[stage][k] + 1 < load[stage][i]:
                        load[stage][k] += 1
                        load[stage][i] -= 1
                        item[4] = i = k
                        moved = True
        self.work = [[[] for _ in range(self.chips)] for _ in range(self.steps + 1)]
        for stage, a, b, _, i in chosen:
            one, two = self.held[i][a], self.held[i][b]
            u, v = (one, two) if one[0] >= two[0] else (two, one)
            self.work[stage][i].append((u[1], v[1]))
        for stage in self.work:
            longest = max(len(pairs) for pairs in stage)
            for pairs in stage:
                while len(pairs) < longest:
                    pairs.append(pairs[-1] if pairs else (0, 0))


def pick(values, index):
    if all(v == values[0] for v in values):
        return jnp.int32(values[0])
    result = jnp.int32(values[-1])
    for i in range(len(values) - 1):
        result = jnp.where(index == i, jnp.int32(values[i]), result)
    return result


def kernel(
    plan, cols, x_ref, o_ref, buf, row_acc, col_acc, parts, got,
    send_sem, recv_sem, side_send, side_recv, part_send, part_recv,
):
    me, core = lax.axis_index("rows"), lax.axis_index("cols")
    chips, steps, own = plan.chips, plan.steps, plan.parts
    rows, width = x_ref.shape
    unit = rows // own
    others = [(k, q) for k in range(chips) for q in range(cols) if (k, q) != (0, 0)]

    def device(k, q):
        return {"rows": lax.rem(me + k, chips), "cols": lax.rem(core + q, cols)}

    barrier = pltpu.get_barrier_semaphore()
    for k, q in others:
        pl.semaphore_signal(barrier, inc=1, device_id=device(k, q), device_id_type=MESH)

    for h in range(own):
        values = x_ref[h * unit:(h + 1) * unit, :].astype(jnp.float32)
        mean = jnp.mean(values * values, axis=1, keepdims=True)
        buf[h, 0] = (values * lax.rsqrt(mean + epsilon) * width ** (-0.5)).astype(jnp.bfloat16)

    pl.semaphore_wait(barrier, len(others))

    def present(table, index):
        return pick([int(v >= 0) for v in table], index) == 1

    def guarded(table, index, action):
        if all(v >= 0 for v in table):
            action()
        elif any(v >= 0 for v in table):
            pl.when(present(table, index))(action)

    def link_copy(d, t):
        slot = own + d * steps + t
        return pltpu.make_async_remote_copy(
            src_ref=buf.at[pick([max(v, 0) for v in plan.source[d][t]], me), 0],
            dst_ref=buf.at[slot, 0],
            send_sem=send_sem.at[d, t],
            recv_sem=recv_sem.at[d, t],
            device_id={"rows": pick([max(v, 0) for v in plan.moves[d]], me), "cols": core},
            device_id_type=MESH,
        )

    def incoming(d, t):
        result = [-1] * chips
        for i in range(chips):
            if plan.source[d][t][i] >= 0:
                result[plan.moves[d][i]] = 1
        return result

    def side_copy(slot, q):
        return pltpu.make_async_remote_copy(
            src_ref=buf.at[slot, 0],
            dst_ref=buf.at[slot, (cols - q) % cols],
            send_sem=side_send.at[slot, q],
            recv_sem=side_recv.at[slot, (cols - q) % cols],
            device_id=device(0, q),
            device_id_type=MESH,
        )

    def start_sends(t):
        for d in range(len(plan.moves)):
            guarded(plan.source[d][t], me, lambda: link_copy(d, t).start())

    def tile(u, v, q, col0, same):
        left = buf[u, 0]
        right = buf[v, q, pl.ds(col0, BLK), :]
        similar = lax.dot_general(
            left, right, (((1,), (1,)), ((), ())), preferred_element_type=jnp.float32
        )
        row_ids = lax.broadcasted_iota(jnp.int32, similar.shape, 0)
        col_ids = lax.broadcasted_iota(jnp.int32, similar.shape, 1) + col0
        limit = jnp.where(same, 0, rows)
        similar = jnp.where(row_ids == col_ids + limit, lowest, similar)
        best = row_acc[u]
        for j in range(BLK // LANES):
            best = jnp.maximum(best, similar[:, j * LANES:(j + 1) * LANES])
        row_acc[u] = best
        tall = jnp.max(similar.reshape(unit // SUBLANES, SUBLANES, BLK), axis=0)
        col_acc[v, q, :, pl.ds(col0, BLK)] = jnp.maximum(col_acc[v, q, :, pl.ds(col0, BLK)], tall)

    def multiply(stage):
        lists = plan.work[stage]
        count = len(lists[0])
        if not count:
            return
        bits = max(plan.slots - 1, 1).bit_length()
        per_word = 30 // (2 * bits)
        words = []
        for first in range(0, count, per_word):
            packed = []
            for i in range(chips):
                word = 0
                for n, (u, v) in enumerate(lists[i][first:first + per_word]):
                    word |= (u | v << bits) << (2 * bits * n)
                packed.append(word)
            words.append(pick(packed, me))
        tiles = unit // BLK

        @pl.loop(0, count * cols * tiles)
        def _(step):
            p, rest = step // (cols * tiles), step % (cols * tiles)
            q, j = rest // tiles, rest % tiles
            word = words[0]
            for n in range(1, len(words)):
                word = jnp.where(p >= n * per_word, words[n], word)
            word = word >> (2 * bits * (p % per_word))
            u, v = word & (2 ** bits - 1), (word >> bits) & (2 ** bits - 1)
            tile(u, v, q, pl.multiple_of(j * BLK, BLK), (u == v) & (q == 0))

    start_sends(0)
    for h in range(own):
        for q in range(1, cols):
            side_copy(h, q).start()
    row_acc[...] = jnp.full(row_acc.shape, lowest, jnp.float32)
    col_acc[...] = jnp.full(col_acc.shape, lowest, jnp.float32)
    parts[...] = jnp.full(parts.shape, lowest, jnp.float32)
    for h in range(own):
        for q in range(1, cols):
            side_copy(h, q).wait_recv()
    multiply(0)
    for t in range(steps):
        for d in range(len(plan.moves)):
            guarded(incoming(d, t), me, lambda: link_copy(d, t).wait_recv())
        if t + 1 < steps:
            start_sends(t + 1)
        for d in range(len(plan.moves)):
            for q in range(1, cols):
                guarded(incoming(d, t), me, lambda: side_copy(own + d * steps + t, q).start())
        for d in range(len(plan.moves)):
            for q in range(1, cols):
                guarded(incoming(d, t), me, lambda: side_copy(own + d * steps + t, q).wait_recv())
        multiply(t + 1)

    for slot in range(plan.slots):
        names = [plan.unit_of[i][slot] for i in range(chips)]
        chip_table = [name[0] if name else -1 for name in names]
        part_table = [name[1] if name else 0 for name in names]

        def fold():
            chip, part = pick([max(v, 0) for v in chip_table], me), pick(part_table, me)
            across = jnp.max(jnp.transpose(row_acc[slot]), axis=0, keepdims=True)
            for q in range(cols):
                best = jnp.max(col_acc[slot, q], axis=0, keepdims=True)
                if q == 0:
                    best = jnp.maximum(best, across)
                place = chip * cols + q
                parts[place, part] = jnp.maximum(parts[place, part], best)

        guarded(chip_table, me, fold)

    def part_copy(k, q):
        return pltpu.make_async_remote_copy(
            src_ref=parts.at[lax.rem(me + k, chips) * cols + q],
            dst_ref=got.at[k * cols + q],
            send_sem=part_send.at[k * cols + q],
            recv_sem=part_recv.at[k * cols + q],
            device_id=device(k, q),
            device_id_type=MESH,
        )

    for k, q in others:
        part_copy(k, q).start()
    result = parts[me * cols]
    for k, q in others:
        part_copy(k, q).wait_recv()
    for k, q in others:
        result = jnp.maximum(result, got[k * cols + q])
    for h in range(own):
        o_ref[:, h * unit:(h + 1) * unit] = result[h]

    for k, q in others:
        part_copy(k, q).wait_send()
    for t in range(steps):
        for d in range(len(plan.moves)):
            guarded(plan.source[d][t], me, lambda: link_copy(d, t).wait_send())
            for q in range(1, cols):
                guarded(incoming(d, t), me, lambda: side_copy(own + d * steps + t, q).wait_send())
    for h in range(own):
        for q in range(1, cols):
            side_copy(h, q).wait_send()


OWN, YNB, LOW, FAR, TOP, PASS, BACK = range(7)
CHUNKS = 8
PIECE = 256
ALL = range(CHUNKS)
HERE, ROUND = range(5 * CHUNKS // 8), range(5 * CHUNKS // 8, CHUNKS)
ROUTES = {
    (0, OWN): [("x", PASS, ROUND), ("u", LOW, ALL), ("y", YNB, ALL)],
    (1, OWN): [("x", BACK, ROUND), ("u", LOW, HERE), ("y", YNB, ALL)],
    (2, OWN): [("y", YNB, ALL)],
    (3, OWN): [("d", TOP, ALL), ("y", YNB, ALL)],
    (3, PASS): [("d", PASS, ROUND)],
    (2, PASS): [("d", PASS, ROUND)],
    (1, PASS): [("x", FAR, ROUND), ("d", PASS, ROUND)],
    (0, PASS): [("x", FAR, ROUND)],
    (2, BACK): [("d", BACK, ROUND)],
    (1, BACK): [("x", LOW, ROUND), ("d", BACK, ROUND)],
    (0, BACK): [("x", LOW, ROUND)],
    (1, LOW): [("u", FAR, HERE)],
    (2, LOW): [("u", LOW, HERE)],
    (2, FAR): [("u", FAR, HERE)],
}
OWNER = {OWN: [0, 1, 2, 3], YNB: [0, 1, 2, 3], LOW: [-1, 0, 1, 1], FAR: [-1, -1, 0, 0], TOP: [-1, -1, 3, -1]}
BUDGET = 6
AHEAD = 2


def target(place, way):
    return {"x": 3 - place, "y": place, "u": place + 1, "d": place - 1}[way]


def relay_plan():
    def depth(place, slot, chunk):
        return max(
            [1 + depth(target(place, way), to, chunk) for way, to, which in ROUTES.get((place, slot), []) if chunk in which],
            default=0,
        )

    queues = {}

    def enqueue(place, slot, chunk, step, order):
        for way, to, which in ROUTES.get((place, slot), []):
            if chunk in which:
                rank = -1 - depth(target(place, way), to, chunk)
                place_in = list(which).index(chunk) if slot == OWN else order
                queues.setdefault((place, way), []).append((rank, place_in, slot, to, chunk, step))

    arrived = {(p, OWN, c): 0 for p in range(4) for c in ALL}
    for p in range(4):
        for c in ALL:
            enqueue(p, OWN, c, 0, c)
    waits, sends, step = [], [], 0
    landing = []
    while landing or any(queues.values()):
        waits.append([[] for _ in range(4)])
        sends.append([[] for _ in range(4)])
        for p, slot, c in landing:
            arrived[p, slot, c] = step
            waits[step][p].append((slot, c))
            enqueue(p, slot, c, step, step)
        landing = []
        for (p, way), queue in queues.items():
            if queue:
                item = min(queue)
                queue.remove(item)
                _, _, slot, to, c, ready = item
                sends[max(ready, step - AHEAD)][p].append((way, slot, to, c))
                landing.append((target(p, way), to, c))
        step += 1
    steps = len(waits)
    share = max(arrived[p, YNB, c] for p in range(4) for c in ALL)
    work = [[[] for _ in range(4)] for _ in range(steps + 1)]
    for p in range(4):
        jobs = []

        def ready(slot, piece):
            per = CHUNKS // PIECES
            return max(arrived[p, slot, c] for c in range(piece * per, piece * per + per))

        for piece in range(PIECES):
            jobs += [(1, (OWN, piece, OWN, q)) for q in range(2)]
            jobs.append((share + 1, (OWN, piece, YNB, 2)))
            for slot in (LOW, FAR, TOP):
                if OWNER[slot][p] >= 0:
                    at = ready(slot, piece)
                    jobs += [(max(1, at), (slot, piece, OWN, q)) for q in range(2)]
                    jobs += [(max(share + 1, at), (slot, piece, YNB, q)) for q in range(2)]
        jobs.sort()
        for t in range(steps + 1):
            able = [j for j in jobs if j[0] <= t]
            take = able if t == steps else able[:BUDGET]
            work[t][p] = [j[1] for j in take]
            jobs = [j for j in jobs if j not in take]
        assert not jobs
    return waits, sends, work, share


PIECES = 512 // PIECE


def relay_kernel(
    x_ref, o_ref, buf, row_acc, col_acc, parts, got,
    send_sem, recv_sem, side_send, side_recv, part_send, part_recv,
):
    waits, sends, work, share = relay_plan()
    group, line, core = lax.axis_index("groups"), lax.axis_index("rows"), lax.axis_index("cols")
    z, y = line // 2, line % 2
    place = z + group * (3 - 2 * z)
    rows, width = x_ref.shape
    chunk_rows = rows // CHUNKS
    upward = 1 - 2 * group

    def neighbour(way):
        if way == "x":
            return {"groups": 1 - group, "rows": line, "cols": core}
        if way == "y":
            return {"groups": group, "rows": 2 * z + 1 - y, "cols": core}
        step = upward if way == "u" else -upward
        return {"groups": group, "rows": line + 2 * step, "cols": core}

    def device_at(at, dy, q):
        zz = at + group * (3 - 2 * at)
        return {"groups": group, "rows": 2 * zz + (y + dy) % 2, "cols": (core + q) % 2}

    barrier = pltpu.get_barrier_semaphore()
    sibling = {"groups": group, "rows": line, "cols": 1 - core}

    def greet(other):
        pl.semaphore_signal(barrier, inc=1, device_id=other, device_id_type=MESH)

    greet(neighbour("x"))
    greet(neighbour("y"))
    greet(sibling)
    pl.when(place < 3)(lambda: greet(neighbour("u")))
    pl.when(place > 0)(lambda: greet(neighbour("d")))

    @pl.loop(0, CHUNKS)
    def _(c):
        at = pl.ds(pl.multiple_of(c * chunk_rows, chunk_rows), chunk_rows)
        values = x_ref[at, :].astype(jnp.float32)
        mean = jnp.mean(values * values, axis=1, keepdims=True)
        buf[OWN, 0, at, :] = (values * lax.rsqrt(mean + epsilon) * width ** (-0.5)).astype(jnp.bfloat16)

    pl.semaphore_wait(barrier, pick([4, 5, 5, 4], place))

    def link_copy(way, slot, to, c, n):
        at = pl.ds(c * chunk_rows, chunk_rows)
        return pltpu.make_async_remote_copy(
            src_ref=buf.at[slot, 0, at],
            dst_ref=buf.at[to, 0, at],
            send_sem=send_sem.at[n],
            recv_sem=recv_sem.at[to, c],
            device_id=neighbour(way),
            device_id_type=MESH,
        )

    def arrival(slot, c):
        return link_copy("x", slot, slot, c, 0)

    def side_copy(n):
        slot = OWN if n == 0 else YNB
        return pltpu.make_async_remote_copy(
            src_ref=buf.at[slot, 0],
            dst_ref=buf.at[slot, 1],
            send_sem=side_send.at[n],
            recv_sem=side_recv.at[n],
            device_id=sibling,
            device_id_type=MESH,
        )

    def multiply(lists):
        longest = max(len(items) for items in lists)
        if not longest:
            return
        packed = [
            [sum((u | piece << 3 | v << 6 | q << 7) << (9 * i) for i, (u, piece, v, q) in enumerate(items[n:n + 3]))
             for items in lists]
            for n in range(0, longest, 3)
        ]
        words = [pick(entry, place) for entry in packed]

        @pl.loop(0, pick([len(items) for items in lists], place))
        def _(n):
            word = words[0]
            for k in range(1, len(words)):
                word = jnp.where(n >= 3 * k, words[k], word)
            word = word >> (9 * (n % 3))
            u, piece, v, q = word & 7, (word >> 3) & 7, (word >> 6) & 1, (word >> 7) & 3
            q = jnp.where(q == 2, y, q)
            at = pl.ds(pl.multiple_of(piece * PIECE, PIECE), PIECE)
            similar = lax.dot_general(
                buf[v, q], buf[u, 0, at, :], (((1,), (1,)), ((), ())), preferred_element_type=jnp.float32
            )
            shift = jnp.where((u == OWN) & (v == OWN) & (q == 0), piece * PIECE, 2 * rows)
            row_ids = lax.broadcasted_iota(jnp.int32, similar.shape, 0)
            col_ids = lax.broadcasted_iota(jnp.int32, similar.shape, 1)
            similar = jnp.where(row_ids - col_ids == shift, lowest, similar)
            best = row_acc[v, q]
            for j in range(PIECE // LANES):
                best = jnp.maximum(best, similar[:, j * LANES:(j + 1) * LANES])
            row_acc[v, q] = best
            tall = jnp.max(similar.reshape(rows // SUBLANES, SUBLANES, PIECE), axis=0)
            col_acc[u, :, at] = jnp.maximum(col_acc[u, :, at], tall)

    steps = len(waits)
    numbers = [0] * 4
    started = [[] for _ in range(4)]
    for t in range(steps):
        if t == 1:
            side_copy(0).wait_recv()
        if t == share + 1:
            side_copy(1).wait_recv()
        for p in range(4):

            @pl.when(place == p)
            def _():
                early = [s for s in sends[t][p] if (s[1], s[3]) not in waits[t][p]]
                for send in early:
                    link_copy(*send, numbers[p]).start()
                    started[p].append((*send, numbers[p]))
                    numbers[p] += 1
                for slot, c in waits[t][p]:
                    arrival(slot, c).wait_recv()
                    for send in sends[t][p]:
                        if (send[1], send[3]) == (slot, c):
                            link_copy(*send, numbers[p]).start()
                            started[p].append((*send, numbers[p]))
                            numbers[p] += 1

        if t == 0:
            side_copy(0).start()
            row_acc[...] = jnp.full(row_acc.shape, lowest, jnp.float32)
            col_acc[...] = jnp.full(col_acc.shape, lowest, jnp.float32)
        if t == share:
            side_copy(1).start()
        multiply(work[t])
    multiply(work[steps])

    for slot in range(TOP + 1):

        def fold(slot=slot):
            down = jnp.max(col_acc[slot], axis=0, keepdims=True)
            if slot <= YNB:
                across = [jnp.max(jnp.transpose(row_acc[slot, q]), axis=0, keepdims=True) for q in range(2)]
                parts[slot, 0] = jnp.maximum(across[0], down)
                parts[slot, 1] = across[1]
            else:
                parts[slot, 0] = down

        if min(OWNER[slot]) >= 0:
            fold()
        else:
            pl.when(present(OWNER[slot], place))(fold)

    def part_copy(slot, p, q):
        n = 2 * slot + q
        dy = 1 if slot == YNB else 0
        return pltpu.make_async_remote_copy(
            src_ref=parts.at[slot, q],
            dst_ref=got.at[p, dy, q],
            send_sem=part_send.at[n],
            recv_sem=part_recv.at[p, dy, q],
            device_id=device_at(OWNER[slot][p], dy, q),
            device_id_type=MESH,
        )

    def messages(p):
        result = [(OWN, 1), (YNB, 0), (YNB, 1)]
        return result + [(slot, 0) for slot in (LOW, FAR, TOP) if OWNER[slot][p] >= 0]

    for p in range(4):

        @pl.when(place == p)
        def _():
            for slot, q in messages(p):
                part_copy(slot, p, q).start()

    o_ref[...] = parts[OWN, 0]
    for p in range(4):

        @pl.when(place == p)
        def _():
            sources = []
            for sender in range(4):
                for slot, q in messages(sender):
                    if OWNER[slot][sender] == p:
                        sources.append((sender, 1 if slot == YNB else 0, q))
                        part_copy(slot, sender, q).wait_recv()
            best = o_ref[...]
            for source in sources:
                best = jnp.maximum(best, got[source])
            o_ref[...] = best
            for slot, q in messages(p):
                part_copy(slot, p, q).wait_send()
            for way, slot, to, c, n in started[p]:
                link_copy(way, slot, to, c, n).wait_send()

    for n in range(2):
        side_copy(n).wait_send()


def present(table, index):
    return pick([int(v >= 0) for v in table], index) == 1


def relayed(embeddings):
    rows, width = embeddings.shape
    best = pl.pallas_call(
        relay_kernel,
        out_shape=jax.ShapeDtypeStruct((1, rows), jnp.float32),
        in_specs=[pl.BlockSpec(memory_space=pltpu.VMEM)],
        out_specs=pl.BlockSpec(memory_space=pltpu.VMEM),
        scratch_shapes=[
            pltpu.VMEM((BACK + 1, 2, rows, width), jnp.bfloat16),
            pltpu.VMEM((2, 2, rows, LANES), jnp.float32),
            pltpu.VMEM((TOP + 1, SUBLANES, rows), jnp.float32),
            pltpu.VMEM((TOP + 1, 2, 1, rows), jnp.float32),
            pltpu.VMEM((4, 2, 2, 1, rows), jnp.float32),
            pltpu.SemaphoreType.DMA((64,)),
            pltpu.SemaphoreType.DMA((BACK + 1, CHUNKS)),
            pltpu.SemaphoreType.DMA((2,)),
            pltpu.SemaphoreType.DMA((2,)),
            pltpu.SemaphoreType.DMA((2 * TOP + 2,)),
            pltpu.SemaphoreType.DMA((4, 2, 2)),
        ],
        compiler_params=pltpu.CompilerParams(
            collective_id=1, has_side_effects=True, vmem_limit_bytes=48 * 2 ** 20
        ),
    )(embeddings)
    return best.reshape(rows)


def shards(embeddings, pair_list, pair_count):
    chips, cols = lax.axis_size("rows"), lax.axis_size("cols")
    rows, width = embeddings.shape
    if (lax.axis_size("groups"), chips, cols) == (2, 8, 2):
        return relayed(embeddings)
    plan = Plan(chips)
    unit = rows // plan.parts
    total = chips * cols
    best = pl.pallas_call(
        functools.partial(kernel, plan, cols),
        out_shape=jax.ShapeDtypeStruct((1, rows), jnp.float32),
        in_specs=[pl.BlockSpec(memory_space=pltpu.VMEM)],
        out_specs=pl.BlockSpec(memory_space=pltpu.VMEM),
        scratch_shapes=[
            pltpu.VMEM((plan.slots, cols, unit, width), jnp.bfloat16),
            pltpu.VMEM((plan.slots, unit, LANES), jnp.float32),
            pltpu.VMEM((plan.slots, cols, SUBLANES, unit), jnp.float32),
            pltpu.VMEM((total, plan.parts, 1, unit), jnp.float32),
            pltpu.VMEM((total, plan.parts, 1, unit), jnp.float32),
            pltpu.SemaphoreType.DMA((len(plan.moves), plan.steps)),
            pltpu.SemaphoreType.DMA((len(plan.moves), plan.steps)),
            pltpu.SemaphoreType.DMA((plan.slots, cols)),
            pltpu.SemaphoreType.DMA((plan.slots, cols)),
            pltpu.SemaphoreType.DMA((total,)),
            pltpu.SemaphoreType.DMA((total,)),
        ],
        compiler_params=pltpu.CompilerParams(
            collective_id=0, has_side_effects=True, vmem_limit_bytes=48 * 2 ** 20
        ),
    )(embeddings)
    return best.reshape(rows)


def solution(mesh):
    in_specs = (
        P(("groups", "rows", "cols"), None),
        P(("rows", "cols"), None, None),
        P(("rows", "cols")),
    )
    out_specs = P(("groups", "rows", "cols"))
    return jax.shard_map(shards, mesh=mesh, in_specs=in_specs, out_specs=out_specs, check_vma=False)
```

```python
import functools
import itertools

import jax
import jax.numpy as jnp
from jax import lax
from jax.experimental import pallas as pl
from jax.experimental.pallas import tpu as pltpu
from jax.sharding import PartitionSpec as P

MESH = pl.DeviceIdType.MESH
BLK = 256
LANES = 128
SUBLANES = 8
lowest = -3.0
epsilon = 1e-06


class Plan:
    def __init__(self, chips):
        self.chips = chips
        self.parts, self.steps = 1, chips // 2
        self.moves = [[(i + 1) % chips for i in range(chips)]]
        self.sends = [[[((i - t) % chips, 0) for i in range(chips)] for t in range(self.steps)]]
        self.slots = self.parts + len(self.moves) * self.steps
        self.unit_of = [[None] * self.slots for _ in range(chips)]
        self.held = [{} for _ in range(chips)]
        for i in range(chips):
            for h in range(self.parts):
                self.unit_of[i][h] = (i, h)
                self.held[i][(i, h)] = (0, h)
        self.source = [[[-1] * chips for _ in range(self.steps)] for _ in self.moves]
        for t in range(self.steps):
            arrived = []
            for d, to in enumerate(self.moves):
                for i in range(chips):
                    unit = self.sends[d][t][i]
                    if unit is None:
                        continue
                    self.source[d][t][i] = self.held[i][unit][1]
                    slot = self.parts + d * self.steps + t
                    self.unit_of[to[i]][slot] = unit
                    arrived.append((to[i], unit, slot))
            for i, unit, slot in arrived:
                self.held[i].setdefault(unit, (t + 1, slot))
        self.assign()

    def assign(self):
        units = [(i, h) for i in range(self.chips) for h in range(self.parts)]
        options = []
        for a, b in itertools.combinations_with_replacement(units, 2):
            places = []
            for i in range(self.chips):
                if a in self.held[i] and b in self.held[i]:
                    places.append((max(self.held[i][a][0], self.held[i][b][0]), i))
            assert places
            first = min(places)[0]
            places = [i for stage, i in places if stage == first]
            options.append((len(places), first, a, b, places))
        options.sort()
        load = [[0] * self.chips for _ in range(self.steps + 1)]
        chosen = []
        for _, stage, a, b, places in options:
            i = min(places, key=lambda k: (load[stage][k], k))
            load[stage][i] += 1
            chosen.append([stage, a, b, places, i])
        moved = True
        while moved:
            moved = False
            for item in chosen:
                stage, a, b, places, i = item
                for k in places:
                    if load[stage][k] + 1 < load[stage][i]:
                        load[stage][k] += 1
                        load[stage][i] -= 1
                        item[4] = i = k
                        moved = True
        self.work = [[[] for _ in range(self.chips)] for _ in range(self.steps + 1)]
        for stage, a, b, _, i in chosen:
            one, two = self.held[i][a], self.held[i][b]
            u, v = (one, two) if one[0] >= two[0] else (two, one)
            self.work[stage][i].append((u[1], v[1]))
        for stage in self.work:
            longest = max(len(pairs) for pairs in stage)
            for pairs in stage:
                while len(pairs) < longest:
                    pairs.append(pairs[-1] if pairs else (0, 0))


def pick(values, index):
    if all(v == values[0] for v in values):
        return jnp.int32(values[0])
    result = jnp.int32(values[-1])
    for i in range(len(values) - 1):
        result = jnp.where(index == i, jnp.int32(values[i]), result)
    return result


def kernel(
    plan, cols, x_ref, o_ref, buf, row_acc, col_acc, parts, got,
    send_sem, recv_sem, side_send, side_recv, part_send, part_recv,
):
    me, core = lax.axis_index("rows"), lax.axis_index("cols")
    chips, steps, own = plan.chips, plan.steps, plan.parts
    rows, width = x_ref.shape
    unit = rows // own
    others = [(k, q) for k in range(chips) for q in range(cols) if (k, q) != (0, 0)]

    def device(k, q):
        return {"rows": lax.rem(me + k, chips), "cols": lax.rem(core + q, cols)}

    barrier = pltpu.get_barrier_semaphore()
    for k, q in others:
        pl.semaphore_signal(barrier, inc=1, device_id=device(k, q), device_id_type=MESH)

    for h in range(own):
        values = x_ref[h * unit:(h + 1) * unit, :].astype(jnp.float32)
        mean = jnp.mean(values * values, axis=1, keepdims=True)
        buf[h, 0] = (values * lax.rsqrt(mean + epsilon) * width ** (-0.5)).astype(jnp.bfloat16)

    pl.semaphore_wait(barrier, len(others))

    def present(table, index):
        return pick([int(v >= 0) for v in table], index) == 1

    def guarded(table, index, action):
        if all(v >= 0 for v in table):
            action()
        elif any(v >= 0 for v in table):
            pl.when(present(table, index))(action)

    def link_copy(d, t):
        slot = own + d * steps + t
        return pltpu.make_async_remote_copy(
            src_ref=buf.at[pick([max(v, 0) for v in plan.source[d][t]], me), 0],
            dst_ref=buf.at[slot, 0],
            send_sem=send_sem.at[d, t],
            recv_sem=recv_sem.at[d, t],
            device_id={"rows": pick([max(v, 0) for v in plan.moves[d]], me), "cols": core},
            device_id_type=MESH,
        )

    def incoming(d, t):
        result = [-1] * chips
        for i in range(chips):
            if plan.source[d][t][i] >= 0:
                result[plan.moves[d][i]] = 1
        return result

    def side_copy(slot, q):
        return pltpu.make_async_remote_copy(
            src_ref=buf.at[slot, 0],
            dst_ref=buf.at[slot, (cols - q) % cols],
            send_sem=side_send.at[slot, q],
            recv_sem=side_recv.at[slot, (cols - q) % cols],
            device_id=device(0, q),
            device_id_type=MESH,
        )

    def start_sends(t):
        for d in range(len(plan.moves)):
            guarded(plan.source[d][t], me, lambda: link_copy(d, t).start())

    def tile(u, v, q, col0, same):
        left = buf[u, 0]
        right = buf[v, q, pl.ds(col0, BLK), :]
        similar = lax.dot_general(
            left, right, (((1,), (1,)), ((), ())), preferred_element_type=jnp.float32
        )
        row_ids = lax.broadcasted_iota(jnp.int32, similar.shape, 0)
        col_ids = lax.broadcasted_iota(jnp.int32, similar.shape, 1) + col0
        limit = jnp.where(same, 0, rows)
        similar = jnp.where(row_ids == col_ids + limit, lowest, similar)
        best = row_acc[u]
        for j in range(BLK // LANES):
            best = jnp.maximum(best, similar[:, j * LANES:(j + 1) * LANES])
        row_acc[u] = best
        tall = jnp.max(similar.reshape(unit // SUBLANES, SUBLANES, BLK), axis=0)
        col_acc[v, q, :, pl.ds(col0, BLK)] = jnp.maximum(col_acc[v, q, :, pl.ds(col0, BLK)], tall)

    def multiply(stage):
        lists = plan.work[stage]
        count = len(lists[0])
        if not count:
            return
        bits = max(plan.slots - 1, 1).bit_length()
        per_word = 30 // (2 * bits)
        words = []
        for first in range(0, count, per_word):
            packed = []
            for i in range(chips):
                word = 0
                for n, (u, v) in enumerate(lists[i][first:first + per_word]):
                    word |= (u | v << bits) << (2 * bits * n)
                packed.append(word)
            words.append(pick(packed, me))
        tiles = unit // BLK

        @pl.loop(0, count * cols * tiles)
        def _(step):
            p, rest = step // (cols * tiles), step % (cols * tiles)
            q, j = rest // tiles, rest % tiles
            word = words[0]
            for n in range(1, len(words)):
                word = jnp.where(p >= n * per_word, words[n], word)
            word = word >> (2 * bits * (p % per_word))
            u, v = word & (2 ** bits - 1), (word >> bits) & (2 ** bits - 1)
            tile(u, v, q, pl.multiple_of(j * BLK, BLK), (u == v) & (q == 0))

    start_sends(0)
    for h in range(own):
        for q in range(1, cols):
            side_copy(h, q).start()
    row_acc[...] = jnp.full(row_acc.shape, lowest, jnp.float32)
    col_acc[...] = jnp.full(col_acc.shape, lowest, jnp.float32)
    parts[...] = jnp.full(parts.shape, lowest, jnp.float32)
    for h in range(own):
        for q in range(1, cols):
            side_copy(h, q).wait_recv()
    multiply(0)
    for t in range(steps):
        for d in range(len(plan.moves)):
            guarded(incoming(d, t), me, lambda: link_copy(d, t).wait_recv())
        if t + 1 < steps:
            start_sends(t + 1)
        for d in range(len(plan.moves)):
            for q in range(1, cols):
                guarded(incoming(d, t), me, lambda: side_copy(own + d * steps + t, q).start())
        for d in range(len(plan.moves)):
            for q in range(1, cols):
                guarded(incoming(d, t), me, lambda: side_copy(own + d * steps + t, q).wait_recv())
        multiply(t + 1)

    for slot in range(plan.slots):
        names = [plan.unit_of[i][slot] for i in range(chips)]
        chip_table = [name[0] if name else -1 for name in names]
        part_table = [name[1] if name else 0 for name in names]

        def fold():
            chip, part = pick([max(v, 0) for v in chip_table], me), pick(part_table, me)
            across = jnp.max(jnp.transpose(row_acc[slot]), axis=0, keepdims=True)
            for q in range(cols):
                best = jnp.max(col_acc[slot, q], axis=0, keepdims=True)
                if q == 0:
                    best = jnp.maximum(best, across)
                place = chip * cols + q
                parts[place, part] = jnp.maximum(parts[place, part], best)

        guarded(chip_table, me, fold)

    def part_copy(k, q):
        return pltpu.make_async_remote_copy(
            src_ref=parts.at[lax.rem(me + k, chips) * cols + q],
            dst_ref=got.at[k * cols + q],
            send_sem=part_send.at[k * cols + q],
            recv_sem=part_recv.at[k * cols + q],
            device_id=device(k, q),
            device_id_type=MESH,
        )

    for k, q in others:
        part_copy(k, q).start()
    result = parts[me * cols]
    for k, q in others:
        part_copy(k, q).wait_recv()
    for k, q in others:
        result = jnp.maximum(result, got[k * cols + q])
    for h in range(own):
        o_ref[:, h * unit:(h + 1) * unit] = result[h]

    for k, q in others:
        part_copy(k, q).wait_send()
    for t in range(steps):
        for d in range(len(plan.moves)):
            guarded(plan.source[d][t], me, lambda: link_copy(d, t).wait_send())
            for q in range(1, cols):
                guarded(incoming(d, t), me, lambda: side_copy(own + d * steps + t, q).wait_send())
    for h in range(own):
        for q in range(1, cols):
            side_copy(h, q).wait_send()


OWN, YNB, LOW, FAR, TOP, PASS, BACK = range(7)
CHUNKS = 8
PIECE = 256
ALL = range(CHUNKS)
HERE, ROUND = range(5 * CHUNKS // 8), range(5 * CHUNKS // 8, CHUNKS)
ROUTES = {
    (0, OWN): [("x", PASS, ROUND), ("u", LOW, ALL), ("y", YNB, ALL)],
    (1, OWN): [("x", BACK, ROUND), ("u", LOW, HERE), ("y", YNB, ALL)],
    (2, OWN): [("y", YNB, ALL)],
    (3, OWN): [("d", TOP, ALL), ("y", YNB, ALL)],
    (3, PASS): [("d", PASS, ROUND)],
    (2, PASS): [("d", PASS, ROUND)],
    (1, PASS): [("x", FAR, ROUND), ("d", PASS, ROUND)],
    (0, PASS): [("x", FAR, ROUND)],
    (2, BACK): [("d", BACK, ROUND)],
    (1, BACK): [("x", LOW, ROUND), ("d", BACK, ROUND)],
    (0, BACK): [("x", LOW, ROUND)],
    (1, LOW): [("u", FAR, HERE)],
    (2, LOW): [("u", LOW, HERE)],
    (2, FAR): [("u", FAR, HERE)],
}
OWNER = {OWN: [0, 1, 2, 3], YNB: [0, 1, 2, 3], LOW: [-1, 0, 1, 1], FAR: [-1, -1, 0, 0], TOP: [-1, -1, 3, -1]}
BUDGET = 4
AHEAD = 2


def target(place, way):
    return {"x": 3 - place, "y": place, "u": place + 1, "d": place - 1}[way]


def relay_plan():
    def depth(place, slot, chunk):
        return max(
            [1 + depth(target(place, way), to, chunk) for way, to, which in ROUTES.get((place, slot), []) if chunk in which],
            default=0,
        )

    queues = {}

    def enqueue(place, slot, chunk, step, order):
        for way, to, which in ROUTES.get((place, slot), []):
            if chunk in which:
                rank = -1 - depth(target(place, way), to, chunk)
                place_in = list(which).index(chunk) if slot == OWN else order
                queues.setdefault((place, way), []).append((rank, place_in, slot, to, chunk, step))

    arrived = {(p, OWN, c): 0 for p in range(4) for c in ALL}
    for p in range(4):
        for c in ALL:
            enqueue(p, OWN, c, 0, c)
    waits, sends, step = [], [], 0
    landing = []
    while landing or any(queues.values()):
        waits.append([[] for _ in range(4)])
        sends.append([[] for _ in range(4)])
        for p, slot, c in landing:
            arrived[p, slot, c] = step
            waits[step][p].append((slot, c))
            enqueue(p, slot, c, step, step)
        landing = []
        for (p, way), queue in queues.items():
            if queue:
                item = min(queue)
                queue.remove(item)
                _, _, slot, to, c, ready = item
                sends[max(ready, step - AHEAD)][p].append((way, slot, to, c))
                landing.append((target(p, way), to, c))
        step += 1
    steps = len(waits)
    share = max(arrived[p, YNB, c] for p in range(4) for c in ALL)
    work = [[[] for _ in range(4)] for _ in range(steps + 1)]
    for p in range(4):
        jobs = []

        def ready(slot, piece):
            per = CHUNKS // PIECES
            return max(arrived[p, slot, c] for c in range(piece * per, piece * per + per))

        for piece in range(PIECES):
            jobs.append((1, (OWN, piece, OWN, 0)))
            for slot in (LOW, FAR, TOP):
                if OWNER[slot][p] >= 0:
                    at = ready(slot, piece)
                    jobs.append((max(1, at), (slot, piece, OWN, 0)))
                    jobs.append((max(share + 1, at), (slot, piece, YNB, 0)))
        jobs.append((share + 1, (OWN, 0, YNB, 1)))
        jobs.sort()
        for t in range(steps + 1):
            able = [j for j in jobs if j[0] <= t]
            take = able if t == steps else able[:BUDGET]
            work[t][p] = [j[1] for j in take]
            jobs = [j for j in jobs if j not in take]
        assert not jobs
    return waits, sends, work, share


PIECES = 512 // PIECE


def relay_kernel(
    x_hbm, o_ref, x_ref, buf, row_acc, col_acc, parts, got,
    load_sem, send_sem, recv_sem, side_send, side_recv, part_send, part_recv,
):
    load = pltpu.make_async_copy(x_hbm, x_ref, load_sem)
    load.start()
    waits, sends, work, share = relay_plan()
    group, line, core = lax.axis_index("groups"), lax.axis_index("rows"), lax.axis_index("cols")
    z, y = line // 2, line % 2
    place = z + group * (3 - 2 * z)
    rows, width = x_ref.shape
    chunk_rows = rows // CHUNKS
    upward = 1 - 2 * group

    def neighbour(way):
        if way == "x":
            return {"groups": 1 - group, "rows": line, "cols": core}
        if way == "y":
            return {"groups": group, "rows": 2 * z + 1 - y, "cols": core}
        step = upward if way == "u" else -upward
        return {"groups": group, "rows": line + 2 * step, "cols": core}

    def device_at(at, dy, q):
        zz = at + group * (3 - 2 * at)
        return {"groups": group, "rows": 2 * zz + (y + dy) % 2, "cols": (core + q) % 2}

    barrier = pltpu.get_barrier_semaphore()
    sibling = {"groups": group, "rows": line, "cols": 1 - core}

    def greet(other):
        pl.semaphore_signal(barrier, inc=1, device_id=other, device_id_type=MESH)

    greet(neighbour("x"))
    greet(neighbour("y"))
    greet(sibling)
    pl.when(place < 3)(lambda: greet(neighbour("u")))
    pl.when(place > 0)(lambda: greet(neighbour("d")))

    load.wait()

    @pl.loop(0, CHUNKS)
    def _(c):
        at = pl.ds(pl.multiple_of(c * chunk_rows, chunk_rows), chunk_rows)
        values = x_ref[at, :].astype(jnp.float32)
        mean = jnp.mean(values * values, axis=1, keepdims=True)
        buf[OWN, 0, at, :] = (values * lax.rsqrt(mean + epsilon) * width ** (-0.5)).astype(jnp.bfloat16)

    pl.semaphore_wait(barrier, pick([4, 5, 5, 4], place))

    def link_copy(way, slot, to, c, n):
        at = pl.ds(c * chunk_rows, chunk_rows)
        return pltpu.make_async_remote_copy(
            src_ref=buf.at[slot, 0, at],
            dst_ref=buf.at[to, 0, at],
            send_sem=send_sem.at[n],
            recv_sem=recv_sem.at[to, c],
            device_id=neighbour(way),
            device_id_type=MESH,
        )

    def arrival(slot, c):
        return link_copy("x", slot, slot, c, 0)

    def side_copy(n):
        slot = OWN if n == 0 else YNB
        return pltpu.make_async_remote_copy(
            src_ref=buf.at[slot, 0],
            dst_ref=buf.at[slot, 1],
            send_sem=side_send.at[n],
            recv_sem=side_recv.at[n],
            device_id=sibling,
            device_id_type=MESH,
        )

    def multiply(lists):
        longest = max(len(items) for items in lists)
        if not longest:
            return
        packed = [
            [sum((u | piece << 3 | v << 6 | q << 7) << (9 * i) for i, (u, piece, v, q) in enumerate(items[n:n + 3]))
             for items in lists]
            for n in range(0, longest, 3)
        ]
        words = [pick(entry, place) for entry in packed]

        @pl.loop(0, pick([len(items) for items in lists], place))
        def _(n):
            word = words[0]
            for k in range(1, len(words)):
                word = jnp.where(n >= 3 * k, words[k], word)
            word = word >> (9 * (n % 3))
            u, piece, v, q = word & 7, (word >> 3) & 7, (word >> 6) & 1, (word >> 7) & 3
            shared = q == 1
            u, piece, v = jnp.where(shared, y, u), jnp.where(shared, y, piece), jnp.where(shared, 1 - y, v)
            at = pl.ds(pl.multiple_of(piece * PIECE, PIECE), PIECE)
            for plane in range(2):
                similar = lax.dot_general(
                    buf[v, plane], buf[u, 0, at, :], (((1,), (1,)), ((), ())), preferred_element_type=jnp.float32
                )
                if plane == 0:
                    shift = jnp.where((u == OWN) & (v == OWN), piece * PIECE, 2 * rows)
                    row_ids = lax.broadcasted_iota(jnp.int32, similar.shape, 0)
                    col_ids = lax.broadcasted_iota(jnp.int32, similar.shape, 1)
                    similar = jnp.where(row_ids - col_ids == shift, lowest, similar)
                best = row_acc[v, plane]
                for j in range(PIECE // LANES):
                    best = jnp.maximum(best, similar[:, j * LANES:(j + 1) * LANES])
                row_acc[v, plane] = best
                tall = jnp.max(similar.reshape(rows // SUBLANES, SUBLANES, PIECE), axis=0)
                col_acc[u, :, at] = jnp.maximum(col_acc[u, :, at], tall)

    steps = len(waits)
    numbers = [0] * 4
    started = [[] for _ in range(4)]
    for t in range(steps):
        if t == 1:
            side_copy(0).wait_recv()
        if t == share + 1:
            side_copy(1).wait_recv()
        for p in range(4):

            @pl.when(place == p)
            def _():
                early = [s for s in sends[t][p] if (s[1], s[3]) not in waits[t][p]]
                for send in early:
                    link_copy(*send, numbers[p]).start()
                    started[p].append((*send, numbers[p]))
                    numbers[p] += 1
                for slot, c in waits[t][p]:
                    arrival(slot, c).wait_recv()
                    for send in sends[t][p]:
                        if (send[1], send[3]) == (slot, c):
                            link_copy(*send, numbers[p]).start()
                            started[p].append((*send, numbers[p]))
                            numbers[p] += 1

        if t == 0:
            side_copy(0).start()
            row_acc[...] = jnp.full(row_acc.shape, lowest, jnp.float32)
            col_acc[...] = jnp.full(col_acc.shape, lowest, jnp.float32)
        if t == share:
            side_copy(1).start()
        multiply(work[t])
    multiply(work[steps])

    for slot in range(TOP + 1):

        def fold(slot=slot):
            down = jnp.max(col_acc[slot], axis=0, keepdims=True)
            if slot <= YNB:
                across = [jnp.max(jnp.transpose(row_acc[slot, q]), axis=0, keepdims=True) for q in range(2)]
                parts[slot, 0] = jnp.maximum(across[0], down)
                parts[slot, 1] = across[1]
            else:
                parts[slot, 0] = down

        if min(OWNER[slot]) >= 0:
            fold()
        else:
            pl.when(present(OWNER[slot], place))(fold)

    def part_copy(slot, p, q):
        n = 2 * slot + q
        dy = 1 if slot == YNB else 0
        return pltpu.make_async_remote_copy(
            src_ref=parts.at[slot, q],
            dst_ref=got.at[p, dy, q],
            send_sem=part_send.at[n],
            recv_sem=part_recv.at[p, dy, q],
            device_id=device_at(OWNER[slot][p], dy, q),
            device_id_type=MESH,
        )

    def messages(p):
        result = [(OWN, 1), (YNB, 0), (YNB, 1)]
        return result + [(slot, 0) for slot in (LOW, FAR, TOP) if OWNER[slot][p] >= 0]

    for p in range(4):

        @pl.when(place == p)
        def _():
            for slot, q in messages(p):
                part_copy(slot, p, q).start()

    o_ref[...] = parts[OWN, 0]
    for p in range(4):

        @pl.when(place == p)
        def _():
            sources = []
            for sender in range(4):
                for slot, q in messages(sender):
                    if OWNER[slot][sender] == p:
                        sources.append((sender, 1 if slot == YNB else 0, q))
                        part_copy(slot, sender, q).wait_recv()
            best = o_ref[...]
            for source in sources:
                best = jnp.maximum(best, got[source])
            o_ref[...] = best
            for slot, q in messages(p):
                part_copy(slot, p, q).wait_send()
            for way, slot, to, c, n in started[p]:
                link_copy(way, slot, to, c, n).wait_send()

    for n in range(2):
        side_copy(n).wait_send()


def present(table, index):
    return pick([int(v >= 0) for v in table], index) == 1


def relayed(embeddings):
    rows, width = embeddings.shape
    best = pl.pallas_call(
        relay_kernel,
        out_shape=jax.ShapeDtypeStruct((1, rows), jnp.float32),
        in_specs=[pl.BlockSpec(memory_space=pl.ANY)],
        out_specs=pl.BlockSpec(memory_space=pltpu.VMEM),
        scratch_shapes=[
            pltpu.VMEM((rows, width), jnp.bfloat16),
            pltpu.VMEM((BACK + 1, 2, rows, width), jnp.bfloat16),
            pltpu.VMEM((2, 2, rows, LANES), jnp.float32),
            pltpu.VMEM((TOP + 1, SUBLANES, rows), jnp.float32),
            pltpu.VMEM((TOP + 1, 2, 1, rows), jnp.float32),
            pltpu.VMEM((4, 2, 2, 1, rows), jnp.float32),
            pltpu.SemaphoreType.DMA,
            pltpu.SemaphoreType.DMA((64,)),
            pltpu.SemaphoreType.DMA((BACK + 1, CHUNKS)),
            pltpu.SemaphoreType.DMA((2,)),
            pltpu.SemaphoreType.DMA((2,)),
            pltpu.SemaphoreType.DMA((2 * TOP + 2,)),
            pltpu.SemaphoreType.DMA((4, 2, 2)),
        ],
        compiler_params=pltpu.CompilerParams(
            collective_id=1, has_side_effects=True, vmem_limit_bytes=48 * 2 ** 20
        ),
    )(embeddings)
    return best.reshape(rows)


def shards(embeddings, pair_list, pair_count):
    chips, cols = lax.axis_size("rows"), lax.axis_size("cols")
    rows, width = embeddings.shape
    if (lax.axis_size("groups"), chips, cols) == (2, 8, 2):
        return relayed(embeddings)
    plan = Plan(chips)
    unit = rows // plan.parts
    total = chips * cols
    best = pl.pallas_call(
        functools.partial(kernel, plan, cols),
        out_shape=jax.ShapeDtypeStruct((1, rows), jnp.float32),
        in_specs=[pl.BlockSpec(memory_space=pltpu.VMEM)],
        out_specs=pl.BlockSpec(memory_space=pltpu.VMEM),
        scratch_shapes=[
            pltpu.VMEM((plan.slots, cols, unit, width), jnp.bfloat16),
            pltpu.VMEM((plan.slots, unit, LANES), jnp.float32),
            pltpu.VMEM((plan.slots, cols, SUBLANES, unit), jnp.float32),
            pltpu.VMEM((total, plan.parts, 1, unit), jnp.float32),
            pltpu.VMEM((total, plan.parts, 1, unit), jnp.float32),
            pltpu.SemaphoreType.DMA((len(plan.moves), plan.steps)),
            pltpu.SemaphoreType.DMA((len(plan.moves), plan.steps)),
            pltpu.SemaphoreType.DMA((plan.slots, cols)),
            pltpu.SemaphoreType.DMA((plan.slots, cols)),
            pltpu.SemaphoreType.DMA((total,)),
            pltpu.SemaphoreType.DMA((total,)),
        ],
        compiler_params=pltpu.CompilerParams(
            collective_id=0, has_side_effects=True, vmem_limit_bytes=48 * 2 ** 20
        ),
    )(embeddings)
    return best.reshape(rows)


def solution(mesh):
    in_specs = (
        P(("groups", "rows", "cols"), None),
        P(("rows", "cols"), None, None),
        P(("rows", "cols")),
    )
    out_specs = P(("groups", "rows", "cols"))
    return jax.shard_map(shards, mesh=mesh, in_specs=in_specs, out_specs=out_specs, check_vma=False)
```

```python
import functools
import itertools

import jax
import jax.numpy as jnp
from jax import lax
from jax.experimental import pallas as pl
from jax.experimental.pallas import tpu as pltpu
from jax.sharding import PartitionSpec as P

MESH = pl.DeviceIdType.MESH
BLK = 256
LANES = 128
SUBLANES = 8
lowest = -3.0
epsilon = 1e-06


class Plan:
    def __init__(self, chips):
        self.chips = chips
        self.parts, self.steps = 1, chips // 2
        self.moves = [[(i + 1) % chips for i in range(chips)]]
        self.sends = [[[((i - t) % chips, 0) for i in range(chips)] for t in range(self.steps)]]
        self.slots = self.parts + len(self.moves) * self.steps
        self.unit_of = [[None] * self.slots for _ in range(chips)]
        self.held = [{} for _ in range(chips)]
        for i in range(chips):
            for h in range(self.parts):
                self.unit_of[i][h] = (i, h)
                self.held[i][(i, h)] = (0, h)
        self.source = [[[-1] * chips for _ in range(self.steps)] for _ in self.moves]
        for t in range(self.steps):
            arrived = []
            for d, to in enumerate(self.moves):
                for i in range(chips):
                    unit = self.sends[d][t][i]
                    if unit is None:
                        continue
                    self.source[d][t][i] = self.held[i][unit][1]
                    slot = self.parts + d * self.steps + t
                    self.unit_of[to[i]][slot] = unit
                    arrived.append((to[i], unit, slot))
            for i, unit, slot in arrived:
                self.held[i].setdefault(unit, (t + 1, slot))
        self.assign()

    def assign(self):
        units = [(i, h) for i in range(self.chips) for h in range(self.parts)]
        options = []
        for a, b in itertools.combinations_with_replacement(units, 2):
            places = []
            for i in range(self.chips):
                if a in self.held[i] and b in self.held[i]:
                    places.append((max(self.held[i][a][0], self.held[i][b][0]), i))
            assert places
            first = min(places)[0]
            places = [i for stage, i in places if stage == first]
            options.append((len(places), first, a, b, places))
        options.sort()
        load = [[0] * self.chips for _ in range(self.steps + 1)]
        chosen = []
        for _, stage, a, b, places in options:
            i = min(places, key=lambda k: (load[stage][k], k))
            load[stage][i] += 1
            chosen.append([stage, a, b, places, i])
        moved = True
        while moved:
            moved = False
            for item in chosen:
                stage, a, b, places, i = item
                for k in places:
                    if load[stage][k] + 1 < load[stage][i]:
                        load[stage][k] += 1
                        load[stage][i] -= 1
                        item[4] = i = k
                        moved = True
        self.work = [[[] for _ in range(self.chips)] for _ in range(self.steps + 1)]
        for stage, a, b, _, i in chosen:
            one, two = self.held[i][a], self.held[i][b]
            u, v = (one, two) if one[0] >= two[0] else (two, one)
            self.work[stage][i].append((u[1], v[1]))
        for stage in self.work:
            longest = max(len(pairs) for pairs in stage)
            for pairs in stage:
                while len(pairs) < longest:
                    pairs.append(pairs[-1] if pairs else (0, 0))


def pick(values, index):
    if all(v == values[0] for v in values):
        return jnp.int32(values[0])
    result = jnp.int32(values[-1])
    for i in range(len(values) - 1):
        result = jnp.where(index == i, jnp.int32(values[i]), result)
    return result


def kernel(
    plan, cols, x_ref, o_ref, buf, row_acc, col_acc, parts, got,
    send_sem, recv_sem, side_send, side_recv, part_send, part_recv,
):
    me, core = lax.axis_index("rows"), lax.axis_index("cols")
    chips, steps, own = plan.chips, plan.steps, plan.parts
    rows, width = x_ref.shape
    unit = rows // own
    others = [(k, q) for k in range(chips) for q in range(cols) if (k, q) != (0, 0)]

    def device(k, q):
        return {"rows": lax.rem(me + k, chips), "cols": lax.rem(core + q, cols)}

    barrier = pltpu.get_barrier_semaphore()
    for k, q in others:
        pl.semaphore_signal(barrier, inc=1, device_id=device(k, q), device_id_type=MESH)

    for h in range(own):
        values = x_ref[h * unit:(h + 1) * unit, :].astype(jnp.float32)
        mean = jnp.mean(values * values, axis=1, keepdims=True)
        buf[h, 0] = (values * lax.rsqrt(mean + epsilon) * width ** (-0.5)).astype(jnp.bfloat16)

    pl.semaphore_wait(barrier, len(others))

    def present(table, index):
        return pick([int(v >= 0) for v in table], index) == 1

    def guarded(table, index, action):
        if all(v >= 0 for v in table):
            action()
        elif any(v >= 0 for v in table):
            pl.when(present(table, index))(action)

    def link_copy(d, t):
        slot = own + d * steps + t
        return pltpu.make_async_remote_copy(
            src_ref=buf.at[pick([max(v, 0) for v in plan.source[d][t]], me), 0],
            dst_ref=buf.at[slot, 0],
            send_sem=send_sem.at[d, t],
            recv_sem=recv_sem.at[d, t],
            device_id={"rows": pick([max(v, 0) for v in plan.moves[d]], me), "cols": core},
            device_id_type=MESH,
        )

    def incoming(d, t):
        result = [-1] * chips
        for i in range(chips):
            if plan.source[d][t][i] >= 0:
                result[plan.moves[d][i]] = 1
        return result

    def side_copy(slot, q):
        return pltpu.make_async_remote_copy(
            src_ref=buf.at[slot, 0],
            dst_ref=buf.at[slot, (cols - q) % cols],
            send_sem=side_send.at[slot, q],
            recv_sem=side_recv.at[slot, (cols - q) % cols],
            device_id=device(0, q),
            device_id_type=MESH,
        )

    def start_sends(t):
        for d in range(len(plan.moves)):
            guarded(plan.source[d][t], me, lambda: link_copy(d, t).start())

    def tile(u, v, q, col0, same):
        left = buf[u, 0]
        right = buf[v, q, pl.ds(col0, BLK), :]
        similar = lax.dot_general(
            left, right, (((1,), (1,)), ((), ())), preferred_element_type=jnp.float32
        )
        row_ids = lax.broadcasted_iota(jnp.int32, similar.shape, 0)
        col_ids = lax.broadcasted_iota(jnp.int32, similar.shape, 1) + col0
        limit = jnp.where(same, 0, rows)
        similar = jnp.where(row_ids == col_ids + limit, lowest, similar)
        best = row_acc[u]
        for j in range(BLK // LANES):
            best = jnp.maximum(best, similar[:, j * LANES:(j + 1) * LANES])
        row_acc[u] = best
        tall = jnp.max(similar.reshape(unit // SUBLANES, SUBLANES, BLK), axis=0)
        col_acc[v, q, :, pl.ds(col0, BLK)] = jnp.maximum(col_acc[v, q, :, pl.ds(col0, BLK)], tall)

    def multiply(stage):
        lists = plan.work[stage]
        count = len(lists[0])
        if not count:
            return
        bits = max(plan.slots - 1, 1).bit_length()
        per_word = 30 // (2 * bits)
        words = []
        for first in range(0, count, per_word):
            packed = []
            for i in range(chips):
                word = 0
                for n, (u, v) in enumerate(lists[i][first:first + per_word]):
                    word |= (u | v << bits) << (2 * bits * n)
                packed.append(word)
            words.append(pick(packed, me))
        tiles = unit // BLK

        @pl.loop(0, count * cols * tiles)
        def _(step):
            p, rest = step // (cols * tiles), step % (cols * tiles)
            q, j = rest // tiles, rest % tiles
            word = words[0]
            for n in range(1, len(words)):
                word = jnp.where(p >= n * per_word, words[n], word)
            word = word >> (2 * bits * (p % per_word))
            u, v = word & (2 ** bits - 1), (word >> bits) & (2 ** bits - 1)
            tile(u, v, q, pl.multiple_of(j * BLK, BLK), (u == v) & (q == 0))

    start_sends(0)
    for h in range(own):
        for q in range(1, cols):
            side_copy(h, q).start()
    row_acc[...] = jnp.full(row_acc.shape, lowest, jnp.float32)
    col_acc[...] = jnp.full(col_acc.shape, lowest, jnp.float32)
    parts[...] = jnp.full(parts.shape, lowest, jnp.float32)
    for h in range(own):
        for q in range(1, cols):
            side_copy(h, q).wait_recv()
    multiply(0)
    for t in range(steps):
        for d in range(len(plan.moves)):
            guarded(incoming(d, t), me, lambda: link_copy(d, t).wait_recv())
        if t + 1 < steps:
            start_sends(t + 1)
        for d in range(len(plan.moves)):
            for q in range(1, cols):
                guarded(incoming(d, t), me, lambda: side_copy(own + d * steps + t, q).start())
        for d in range(len(plan.moves)):
            for q in range(1, cols):
                guarded(incoming(d, t), me, lambda: side_copy(own + d * steps + t, q).wait_recv())
        multiply(t + 1)

    for slot in range(plan.slots):
        names = [plan.unit_of[i][slot] for i in range(chips)]
        chip_table = [name[0] if name else -1 for name in names]
        part_table = [name[1] if name else 0 for name in names]

        def fold():
            chip, part = pick([max(v, 0) for v in chip_table], me), pick(part_table, me)
            across = jnp.max(jnp.transpose(row_acc[slot]), axis=0, keepdims=True)
            for q in range(cols):
                best = jnp.max(col_acc[slot, q], axis=0, keepdims=True)
                if q == 0:
                    best = jnp.maximum(best, across)
                place = chip * cols + q
                parts[place, part] = jnp.maximum(parts[place, part], best)

        guarded(chip_table, me, fold)

    def part_copy(k, q):
        return pltpu.make_async_remote_copy(
            src_ref=parts.at[lax.rem(me + k, chips) * cols + q],
            dst_ref=got.at[k * cols + q],
            send_sem=part_send.at[k * cols + q],
            recv_sem=part_recv.at[k * cols + q],
            device_id=device(k, q),
            device_id_type=MESH,
        )

    for k, q in others:
        part_copy(k, q).start()
    result = parts[me * cols]
    for k, q in others:
        part_copy(k, q).wait_recv()
    for k, q in others:
        result = jnp.maximum(result, got[k * cols + q])
    for h in range(own):
        o_ref[:, h * unit:(h + 1) * unit] = result[h]

    for k, q in others:
        part_copy(k, q).wait_send()
    for t in range(steps):
        for d in range(len(plan.moves)):
            guarded(plan.source[d][t], me, lambda: link_copy(d, t).wait_send())
            for q in range(1, cols):
                guarded(incoming(d, t), me, lambda: side_copy(own + d * steps + t, q).wait_send())
    for h in range(own):
        for q in range(1, cols):
            side_copy(h, q).wait_send()


OWN, YNB, LOW, FAR, TOP, PASS, BACK = range(7)
CHUNKS = 8
PIECE = 256
ALL = range(CHUNKS)
HERE, ROUND = range(5 * CHUNKS // 8), range(5 * CHUNKS // 8, CHUNKS)
ROUTES = {
    (0, OWN): [("x", PASS, ROUND), ("u", LOW, ALL), ("y", YNB, ALL)],
    (1, OWN): [("x", BACK, ROUND), ("u", LOW, HERE), ("y", YNB, ALL)],
    (2, OWN): [("y", YNB, ALL)],
    (3, OWN): [("d", TOP, ALL), ("y", YNB, ALL)],
    (3, PASS): [("d", PASS, ROUND)],
    (2, PASS): [("d", PASS, ROUND)],
    (1, PASS): [("x", FAR, ROUND), ("d", PASS, ROUND)],
    (0, PASS): [("x", FAR, ROUND)],
    (2, BACK): [("d", BACK, ROUND)],
    (1, BACK): [("x", LOW, ROUND), ("d", BACK, ROUND)],
    (0, BACK): [("x", LOW, ROUND)],
    (1, LOW): [("u", FAR, HERE)],
    (2, LOW): [("u", LOW, HERE)],
    (2, FAR): [("u", FAR, HERE)],
}
OWNER = {OWN: [0, 1, 2, 3], YNB: [0, 1, 2, 3], LOW: [-1, 0, 1, 1], FAR: [-1, -1, 0, 0], TOP: [-1, -1, 3, -1]}
BUDGET = 4
AHEAD = 2


def target(place, way):
    return {"x": 3 - place, "y": place, "u": place + 1, "d": place - 1}[way]


def relay_plan():
    def depth(place, slot, chunk):
        return max(
            [1 + depth(target(place, way), to, chunk) for way, to, which in ROUTES.get((place, slot), []) if chunk in which],
            default=0,
        )

    queues = {}

    def enqueue(place, slot, chunk, step, order):
        for way, to, which in ROUTES.get((place, slot), []):
            if chunk in which:
                rank = -1 - depth(target(place, way), to, chunk)
                place_in = list(which).index(chunk) if slot == OWN else order
                queues.setdefault((place, way), []).append((rank, place_in, slot, to, chunk, step))

    arrived = {(p, OWN, c): 0 for p in range(4) for c in ALL}
    for p in range(4):
        for c in ALL:
            enqueue(p, OWN, c, 0, c)
    waits, sends, step = [], [], 0
    landing = []
    while landing or any(queues.values()):
        waits.append([[] for _ in range(4)])
        sends.append([[] for _ in range(4)])
        for p, slot, c in landing:
            arrived[p, slot, c] = step
            waits[step][p].append((slot, c))
            enqueue(p, slot, c, step, step)
        landing = []
        for (p, way), queue in queues.items():
            if queue:
                item = min(queue)
                queue.remove(item)
                _, _, slot, to, c, ready = item
                sends[max(ready, step - AHEAD)][p].append((way, slot, to, c))
                landing.append((target(p, way), to, c))
        step += 1
    steps = len(waits)
    share = max(arrived[p, YNB, c] for p in range(4) for c in ALL)
    work = [[[] for _ in range(4)] for _ in range(steps + 1)]
    for p in range(4):
        jobs = []

        def ready(slot, piece):
            per = CHUNKS // PIECES
            return max(arrived[p, slot, c] for c in range(piece * per, piece * per + per))

        for piece in range(PIECES):
            jobs.append((1, (OWN, piece, OWN, 0)))
            for slot in (LOW, FAR, TOP):
                if OWNER[slot][p] >= 0:
                    at = ready(slot, piece)
                    jobs.append((max(1, at), (slot, piece, OWN, 0)))
                    jobs.append((max(share + 1, at), (slot, piece, YNB, 0)))
        jobs.append((share + 1, (OWN, 0, YNB, 1)))
        jobs.sort()
        for t in range(steps + 1):
            able = [j for j in jobs if j[0] <= t]
            take = able if t == steps else able[:BUDGET]
            work[t][p] = [j[1] for j in take]
            jobs = [j for j in jobs if j not in take]
        assert not jobs
    return waits, sends, work, share


PIECES = 512 // PIECE


def relay_kernel(
    x_hbm, o_ref, x_ref, buf, row_acc, col_acc, parts, got,
    load_sem, send_sem, recv_sem, side_send, side_recv, part_send, part_recv,
):
    load = pltpu.make_async_copy(x_hbm, x_ref, load_sem)
    load.start()
    waits, sends, work, share = relay_plan()
    group, line, core = lax.axis_index("groups"), lax.axis_index("rows"), lax.axis_index("cols")
    z, y = line // 2, line % 2
    place = z + group * (3 - 2 * z)
    rows, width = x_ref.shape
    chunk_rows = rows // CHUNKS
    upward = 1 - 2 * group

    def neighbour(way):
        if way == "x":
            return {"groups": 1 - group, "rows": line, "cols": core}
        if way == "y":
            return {"groups": group, "rows": 2 * z + 1 - y, "cols": core}
        step = upward if way == "u" else -upward
        return {"groups": group, "rows": line + 2 * step, "cols": core}

    def device_at(at, dy, q):
        zz = at + group * (3 - 2 * at)
        return {"groups": group, "rows": 2 * zz + (y + dy) % 2, "cols": (core + q) % 2}

    barrier = pltpu.get_barrier_semaphore()
    sibling = {"groups": group, "rows": line, "cols": 1 - core}

    def greet(other):
        pl.semaphore_signal(barrier, inc=1, device_id=other, device_id_type=MESH)

    greet(neighbour("x"))
    greet(neighbour("y"))
    greet(sibling)
    pl.when(place < 3)(lambda: greet(neighbour("u")))
    pl.when(place > 0)(lambda: greet(neighbour("d")))

    load.wait()

    @pl.loop(0, CHUNKS)
    def _(c):
        at = pl.ds(pl.multiple_of(c * chunk_rows, chunk_rows), chunk_rows)
        values = x_ref[at, :].astype(jnp.float32)
        mean = jnp.mean(values * values, axis=1, keepdims=True)
        buf[OWN, 0, at, :] = (values * lax.rsqrt(mean + epsilon) * width ** (-0.5)).astype(jnp.bfloat16)

    pl.semaphore_wait(barrier, pick([4, 5, 5, 4], place))

    def link_copy(way, slot, to, c, n):
        at = pl.ds(c * chunk_rows, chunk_rows)
        return pltpu.make_async_remote_copy(
            src_ref=buf.at[slot, 0, at],
            dst_ref=buf.at[to, 0, at],
            send_sem=send_sem.at[n],
            recv_sem=recv_sem.at[to, c],
            device_id=neighbour(way),
            device_id_type=MESH,
        )

    def arrival(slot, c):
        return link_copy("x", slot, slot, c, 0)

    def side_copy(n):
        slot = OWN if n == 0 else YNB
        return pltpu.make_async_remote_copy(
            src_ref=buf.at[slot, 0],
            dst_ref=buf.at[slot, 1],
            send_sem=side_send.at[n],
            recv_sem=side_recv.at[n],
            device_id=sibling,
            device_id_type=MESH,
        )

    def multiply(lists):
        longest = max(len(items) for items in lists)
        if not longest:
            return
        packed = [
            [sum((u | piece << 3 | v << 6 | q << 7) << (9 * i) for i, (u, piece, v, q) in enumerate(items[n:n + 3]))
             for items in lists]
            for n in range(0, longest, 3)
        ]
        words = [pick(entry, place) for entry in packed]

        @pl.loop(0, pick([len(items) for items in lists], place))
        def _(n):
            word = words[0]
            for k in range(1, len(words)):
                word = jnp.where(n >= 3 * k, words[k], word)
            word = word >> (9 * (n % 3))
            u, piece, v, q = word & 7, (word >> 3) & 7, (word >> 6) & 1, (word >> 7) & 3
            shared = q == 1
            u, piece, v = jnp.where(shared, y, u), jnp.where(shared, y, piece), jnp.where(shared, 1 - y, v)
            at = pl.ds(pl.multiple_of(piece * PIECE, PIECE), PIECE)
            for plane in range(2):
                similar = lax.dot_general(
                    buf[v, plane], buf[u, 0, at, :], (((1,), (1,)), ((), ())), preferred_element_type=jnp.float32
                )
                if plane == 0:
                    shift = jnp.where((u == OWN) & (v == OWN), piece * PIECE, 2 * rows)
                    row_ids = lax.broadcasted_iota(jnp.int32, similar.shape, 0)
                    col_ids = lax.broadcasted_iota(jnp.int32, similar.shape, 1)
                    similar = jnp.where(row_ids - col_ids == shift, lowest, similar)
                best = row_acc[v, plane]
                for j in range(PIECE // LANES):
                    best = jnp.maximum(best, similar[:, j * LANES:(j + 1) * LANES])
                row_acc[v, plane] = best
                tall = jnp.max(similar.reshape(rows // SUBLANES, SUBLANES, PIECE), axis=0)
                col_acc[u, :, at] = jnp.maximum(col_acc[u, :, at], tall)

    steps = len(waits)
    numbers = [0] * 4
    started = [[] for _ in range(4)]
    for t in range(steps):
        if t == 1:
            side_copy(0).wait_recv()
        if t == share + 1:
            side_copy(1).wait_recv()
        for p in range(4):

            @pl.when(place == p)
            def _():
                early = [s for s in sends[t][p] if (s[1], s[3]) not in waits[t][p]]
                for send in early:
                    link_copy(*send, numbers[p]).start()
                    started[p].append((*send, numbers[p]))
                    numbers[p] += 1
                for slot, c in waits[t][p]:
                    arrival(slot, c).wait_recv()
                    for send in sends[t][p]:
                        if (send[1], send[3]) == (slot, c):
                            link_copy(*send, numbers[p]).start()
                            started[p].append((*send, numbers[p]))
                            numbers[p] += 1

        if t == 0:
            side_copy(0).start()
            row_acc[...] = jnp.full(row_acc.shape, lowest, jnp.float32)
            col_acc[...] = jnp.full(col_acc.shape, lowest, jnp.float32)
        if t == share:
            side_copy(1).start()
        multiply(work[t])
    multiply(work[steps])

    def part_copy(slot, p, q):
        n = 2 * slot + q
        dy = 1 if slot == YNB else 0
        return pltpu.make_async_remote_copy(
            src_ref=parts.at[slot, q],
            dst_ref=got.at[p, dy, q],
            send_sem=part_send.at[n],
            recv_sem=part_recv.at[p, dy, q],
            device_id=device_at(OWNER[slot][p], dy, q),
            device_id_type=MESH,
        )

    def messages(p):
        result = [(OWN, 1), (YNB, 0), (YNB, 1)]
        return result + [(slot, 0) for slot in (LOW, FAR, TOP) if OWNER[slot][p] >= 0]

    for slot in (LOW, FAR, TOP, YNB, OWN):

        def fold(slot=slot):
            down = jnp.max(col_acc[slot], axis=0, keepdims=True)
            if slot <= YNB:
                across = [jnp.max(jnp.transpose(row_acc[slot, q]), axis=0, keepdims=True) for q in range(2)]
                parts[slot, 0] = jnp.maximum(across[0], down)
                parts[slot, 1] = across[1]
            else:
                parts[slot, 0] = down

        if min(OWNER[slot]) >= 0:
            fold()
        else:
            pl.when(present(OWNER[slot], place))(fold)
        if slot in (TOP, YNB, OWN):
            for p in range(4):

                @pl.when(place == p)
                def _():
                    for item, q in messages(p):
                        if item == slot or (slot == TOP and item > YNB):
                            part_copy(item, p, q).start()

    o_ref[...] = parts[OWN, 0]
    for p in range(4):

        @pl.when(place == p)
        def _():
            sources = []
            for sender in range(4):
                for slot, q in messages(sender):
                    if OWNER[slot][sender] == p:
                        sources.append((sender, 1 if slot == YNB else 0, q))
                        part_copy(slot, sender, q).wait_recv()
            best = o_ref[...]
            for source in sources:
                best = jnp.maximum(best, got[source])
            o_ref[...] = best
            for slot, q in messages(p):
                part_copy(slot, p, q).wait_send()
            for way, slot, to, c, n in started[p]:
                link_copy(way, slot, to, c, n).wait_send()

    for n in range(2):
        side_copy(n).wait_send()


def present(table, index):
    return pick([int(v >= 0) for v in table], index) == 1


def relayed(embeddings):
    rows, width = embeddings.shape
    best = pl.pallas_call(
        relay_kernel,
        out_shape=jax.ShapeDtypeStruct((1, rows), jnp.float32),
        in_specs=[pl.BlockSpec(memory_space=pl.ANY)],
        out_specs=pl.BlockSpec(memory_space=pltpu.VMEM),
        scratch_shapes=[
            pltpu.VMEM((rows, width), jnp.bfloat16),
            pltpu.VMEM((BACK + 1, 2, rows, width), jnp.bfloat16),
            pltpu.VMEM((2, 2, rows, LANES), jnp.float32),
            pltpu.VMEM((TOP + 1, SUBLANES, rows), jnp.float32),
            pltpu.VMEM((TOP + 1, 2, 1, rows), jnp.float32),
            pltpu.VMEM((4, 2, 2, 1, rows), jnp.float32),
            pltpu.SemaphoreType.DMA,
            pltpu.SemaphoreType.DMA((64,)),
            pltpu.SemaphoreType.DMA((BACK + 1, CHUNKS)),
            pltpu.SemaphoreType.DMA((2,)),
            pltpu.SemaphoreType.DMA((2,)),
            pltpu.SemaphoreType.DMA((2 * TOP + 2,)),
            pltpu.SemaphoreType.DMA((4, 2, 2)),
        ],
        compiler_params=pltpu.CompilerParams(
            collective_id=1, has_side_effects=True, vmem_limit_bytes=48 * 2 ** 20
        ),
    )(embeddings)
    return best.reshape(rows)


def shards(embeddings, pair_list, pair_count):
    chips, cols = lax.axis_size("rows"), lax.axis_size("cols")
    rows, width = embeddings.shape
    if (lax.axis_size("groups"), chips, cols) == (2, 8, 2):
        return relayed(embeddings)
    plan = Plan(chips)
    unit = rows // plan.parts
    total = chips * cols
    best = pl.pallas_call(
        functools.partial(kernel, plan, cols),
        out_shape=jax.ShapeDtypeStruct((1, rows), jnp.float32),
        in_specs=[pl.BlockSpec(memory_space=pltpu.VMEM)],
        out_specs=pl.BlockSpec(memory_space=pltpu.VMEM),
        scratch_shapes=[
            pltpu.VMEM((plan.slots, cols, unit, width), jnp.bfloat16),
            pltpu.VMEM((plan.slots, unit, LANES), jnp.float32),
            pltpu.VMEM((plan.slots, cols, SUBLANES, unit), jnp.float32),
            pltpu.VMEM((total, plan.parts, 1, unit), jnp.float32),
            pltpu.VMEM((total, plan.parts, 1, unit), jnp.float32),
            pltpu.SemaphoreType.DMA((len(plan.moves), plan.steps)),
            pltpu.SemaphoreType.DMA((len(plan.moves), plan.steps)),
            pltpu.SemaphoreType.DMA((plan.slots, cols)),
            pltpu.SemaphoreType.DMA((plan.slots, cols)),
            pltpu.SemaphoreType.DMA((total,)),
            pltpu.SemaphoreType.DMA((total,)),
        ],
        compiler_params=pltpu.CompilerParams(
            collective_id=0, has_side_effects=True, vmem_limit_bytes=48 * 2 ** 20
        ),
    )(embeddings)
    return best.reshape(rows)


def solution(mesh):
    in_specs = (
        P(("groups", "rows", "cols"), None),
        P(("rows", "cols"), None, None),
        P(("rows", "cols")),
    )
    out_specs = P(("groups", "rows", "cols"))
    return jax.shard_map(shards, mesh=mesh, in_specs=in_specs, out_specs=out_specs, check_vma=False)
```
